128 devices in a mesh: expert: 64 (over z, y, x), replica: 2 (over core).
Axes of the slice: x: 4, y: 4, z: 4, core: 2. Of those that a mesh axis runs over, the one named last changes fastest.
Arguments:
- samples: float32 [131072, 256], P(('expert', 'replica')), may hold values from -6 to 6
- routes: int32 [131072, 1], P(('expert', 'replica')), may hold values from 0 to 63; in each aligned block of 1024 rows (0 to 1023, 1024 to 2047, ...) at most 32 rows name the same one
- cotangent: float32 [131072, 256], P(('expert', 'replica')), may hold values from -6 to 6
- weights: float32 [7, 64, 256, 256], P(None, 'expert', 'replica'), may hold values from -0.375 to 0.375
- moment_one: float32 [7, 64, 256, 256], P(None, 'expert', 'replica'), may hold values from -6 to 6
- moment_two: float32 [7, 64, 256, 256], P(None, 'expert', 'replica'), may hold values from 1 to 30
Outputs:
- outputs: float32 [131072, 256], P(('expert', 'replica'))
- new_weights: float32 [7, 64, 256, 256], P(None, 'expert', 'replica')
- new_moment_one: float32 [7, 64, 256, 256], P(None, 'expert', 'replica')
- new_moment_two: float32 [7, 64, 256, 256], P(None, 'expert', 'replica')
The draws below stay inside these ranges and needn't reach their ends.
Inputs may be any that keep to these rules, and one draw needn't show every extreme that they name: `routes`: among the 1024 rows of one device no expert is chosen by more than 32 rows; some expert is chosen by exactly 32 rows of some device.
All inputs are finite; a program needn't handle non-finite values.
Results may differ from the reference program's by a relative error of at most 0.0002.
Values sent between devices are 32-bit elements; how exact they have to be, the bound alone decides.
A program may use at most 128 MiB of HBM per device.

```python
import math
import jax
import jax.numpy as jnp
import numpy as np
from jax import lax

D = 256
LAYERS = 7
TOK_DEV = 1024
EXPERTS = 64
CAP = 32
ROWS = 131072
DEVICES = 128


def block_levels(stream_key, extent, pieces, low, largest):
    factor_of = 1.0
    for axis_at, blocks in pieces:
        steps = jax.random.uniform(jax.random.fold_in(jax.random.fold_in(stream_key, 6), axis_at), (blocks,), jnp.float32, low / len(pieces), largest / len(pieces))
        factor_of = factor_of * jnp.repeat(jnp.exp(steps), extent[axis_at] // blocks).reshape((-1,) + (1,) * (len(extent) - 1 - axis_at))
    return factor_of


def routed_block(stream_key, own, number, rows, count, top, bound, lean):
    sequence = jax.random.permutation(stream_key, count)
    crowded, usual = load_shares(count, rows * top, bound, lean, True), load_shares(count, rows * top, bound, lean, False)
    places = jnp.arange(count)

    def named(tallies, turn):
        used = int((tallies > 0).sum())
        fixed = max(1, used // 4)
        shifted = fixed + (places - fixed + turn * (used - fixed)) % max(1, count - fixed)
        return jnp.zeros((count,), jnp.int32).at[sequence[jnp.where(places < fixed, places, shifted)]].set(jnp.asarray(tallies, jnp.int32))

    tallies = jnp.where(number % 4 == 0, named(crowded, number // 4), named(usual, number - number // 4 - 1))
    mixed = jax.random.permutation(jax.random.fold_in(own, 3), count)
    giver, receiver = mixed[0:count // 2 * 2:2], mixed[1:count // 2 * 2:2]
    slack = jnp.minimum(tallies[giver] - 1, bound - tallies[receiver]) // 2
    slack = jnp.where((giver == sequence[0]) | (receiver == sequence[0]) | (tallies[receiver] == 0), 0, jnp.maximum(slack, 0))
    shifted = jax.random.randint(jax.random.fold_in(own, 4), (count // 2,), 0, 1 << 20) % (slack + 1)
    tallies = tallies.at[giver].add(-shifted).at[receiver].add(shifted)
    items = jnp.searchsorted(jnp.cumsum(tallies), jnp.arange(rows * top), side="right").astype(jnp.int32)
    listing = items.reshape(top, rows).T
    listing = listing[jax.random.permutation(jax.random.fold_in(own, 1), rows)]
    turn = jax.random.randint(jax.random.fold_in(own, 2), (rows, 1), 0, top)
    return jnp.take_along_axis(listing, (jnp.arange(top)[None, :] + turn) % top, axis=1)


def load_shares(count, total, reach, skew, full):
    loads = [(1 << 20) // math.isqrt(grade ** skew) + 1 for grade in range(1, count + 1)]
    largest = reach if full else min(reach, max(-(-total // count), total * loads[0] // sum(loads)))
    least = 1 if total - largest >= count - 1 else 0
    given, spare = [largest] + [least] * (count - 1), total - largest - least * (count - 1)
    while spare > 0:
        candidates = [i for i in range(1, count) if given[i] < largest] or [i for i in range(1, count) if given[i] < reach]
        pool, remaining = sum([loads[i] for i in candidates]), spare
        for i in candidates:
            more = min(reach - given[i], max(1, remaining * loads[i] // pool), spare)
            given[i] = given[i] + more
            spare = spare - more
    return np.array(given)


def normal_values(stream_key, dims, scale, limit, pieces=(), kind=jnp.bfloat16):
    entries = scale * jax.random.normal(stream_key, dims, jnp.float32)
    if pieces:
        entries = entries * block_levels(stream_key, dims, pieces, -0.22, 0.18)
    return jnp.clip(entries, -limit, limit).astype(kind)


def setup_inputs(seed: int = 0) -> dict:
    keys = jax.random.split(jax.random.key(seed), 7)
    samples = normal_values(keys[0], (ROWS, D), 1.0, 6.0, ((0, 128),), jnp.float32)
    routes_keys = jax.random.split(jax.random.fold_in(keys[1], 1), ROWS // TOK_DEV)
    routes_turns = jax.random.permutation(jax.random.fold_in(keys[1], 3), ROWS // TOK_DEV)
    routes = jax.vmap(lambda own, number: routed_block(jax.random.fold_in(keys[1], 2), own, number, TOK_DEV, EXPERTS, 1, CAP, 2))(routes_keys, routes_turns).reshape((ROWS, 1))
    cotangent = normal_values(keys[2], (ROWS, D), 1.0, 6.0, ((0, 128),), jnp.float32)
    weights = normal_values(keys[3], (LAYERS, EXPERTS, D, D), D ** -0.5, 0.375, ((1, 64), (2, 2)), jnp.float32)
    moment_one = normal_values(keys[4], (LAYERS, EXPERTS, D, D), 1.0, 6.0, ((1, 64), (2, 2)), jnp.float32)
    moment_two = jnp.clip(jnp.exp(math.log(30.0) - 3.4011974 * jax.random.uniform(keys[5], (LAYERS, EXPERTS, D, D), jnp.float32) ** block_levels(keys[5], (LAYERS, EXPERTS, D, D), ((1, 64), (2, 2)), -0.2, 0.2)), 1.0, 30.0)
    return {"samples": samples, "routes": routes, "cotangent": cotangent, "weights": weights, "moment_one": moment_one, "moment_two": moment_two}


HIGH = lax.Precision.HIGHEST
CORR_ONE = 0.9999734386011124
CORR_TWO = 0.09520785288629038

def silu_slope(value):
    sigma = jax.nn.sigmoid(value)
    return sigma * (1.0 + value * (1.0 - sigma))

def expert_pass(inputs):
    rows, grads_in, mats = inputs
    acts = []
    pres = []
    hidden = rows
    for layer in range(LAYERS):
        acts.append(hidden)
        pre = jnp.dot(hidden, mats[layer], precision=HIGH, preferred_element_type=jnp.float32)
        pres.append(pre)
        if layer < LAYERS - 1:
            hidden = pre * jax.nn.sigmoid(pre)
    delta = grads_in
    grads = [None] * LAYERS
    for layer in range(LAYERS - 1, -1, -1):
        grads[layer] = lax.dot_general(acts[layer], delta, (((0,), (0,)), ((), ())), precision=HIGH, preferred_element_type=jnp.float32)
        if layer > 0:
            back = lax.dot_general(delta, mats[layer], (((1,), (1,)), ((), ())), precision=HIGH, preferred_element_type=jnp.float32)
            delta = back * silu_slope(pres[layer - 1])
    return (pres[LAYERS - 1], jnp.stack(grads))

def reference(samples, routes, cotangent, weights, moment_one, moment_two):
    route = routes[:, 0].astype(jnp.int32)
    blocked = route.reshape(DEVICES, TOK_DEV)
    onehot = (blocked[:, :, None] == jnp.arange(EXPERTS, dtype=jnp.int32)[None, None, :]).astype(jnp.int32)
    before = jnp.cumsum(onehot, axis=1) - onehot
    rank = lax.optimization_barrier(jnp.sum(before * onehot, axis=2)).reshape(-1)
    source = (jnp.arange(DEVICES * TOK_DEV, dtype=jnp.int32) // TOK_DEV).astype(jnp.int32)
    slot = route * (DEVICES * CAP) + source * CAP + rank
    total = EXPERTS * DEVICES * CAP
    packed = jnp.zeros((total, D), jnp.float32).at[slot].set(samples).reshape(EXPERTS, DEVICES * CAP, D)
    packed_cot = jnp.zeros((total, D), jnp.float32).at[slot].set(cotangent).reshape(EXPERTS, DEVICES * CAP, D)
    mats = jnp.transpose(weights, (1, 0, 2, 3))
    results, grads = lax.map(expert_pass, (packed, packed_cot, mats))
    outputs = results.reshape(total, D)[slot]
    grad = jnp.transpose(grads, (1, 0, 2, 3))
    new_one = 0.9 * moment_one + 0.1 * grad
    new_two = 0.999 * moment_two + 0.001 * grad * grad
    new_w = weights - 0.01 * (new_one / CORR_ONE) / (jnp.sqrt(new_two / CORR_TWO) + 1e-08)
    return (outputs, new_w, new_one, new_two)
```

```python
import jax
import jax.numpy as jnp
from jax import lax
from jax.experimental import pallas as pl
from jax.experimental.pallas import tpu as pltpu
from jax.sharding import PartitionSpec as P

MESH = pl.DeviceIdType.MESH
CORR_ONE = 0.9999734386011124
CORR_TWO = 0.09520785288629038
F32 = jnp.float32
BF16 = jnp.bfloat16

SIDE = 4
PEERS = SIDE**3
CAP = 32
WIDTH = 256
ROWS = 1024
LAYERS = 7
HALF = WIDTH // 2
PER = 8
GROUPS = PEERS // PER
TILE = PER * CAP
STRIDE = 37


def split(value):
    high = value.astype(BF16)
    low = (value - high.astype(F32)).astype(BF16)
    return high, low


def mm(a, b):
    return lax.dot_general(a, b, (((1,), (0,)), ((), ())), preferred_element_type=F32)


def mm_nt(a, b):
    return lax.dot_general(a, b, (((1,), (1,)), ((), ())), preferred_element_type=F32)


def mm_tn(a, b):
    return lax.dot_general(a, b, (((0,), (0,)), ((), ())), preferred_element_type=F32)


def peer(me, k):
    off = (k * STRIDE) % PEERS
    x = (me + off) % SIDE
    y = (me // SIDE + off // SIDE) % SIDE
    z = (me // (SIDE * SIDE) + off // (SIDE * SIDE)) % SIDE
    return z * (SIDE * SIDE) + y * SIDE + x


def peer_back(me, k):
    off = (k * STRIDE) % PEERS
    x = (me + SIDE - off % SIDE) % SIDE
    y = (me // SIDE + SIDE - (off // SIDE) % SIDE) % SIDE
    z = (me // (SIDE * SIDE) + SIDE - off // (SIDE * SIDE)) % SIDE
    return z * (SIDE * SIDE) + y * SIDE + x


def wanted(me, group, shape, axis):
    j = lax.broadcasted_iota(jnp.int32, shape, axis) + group * TILE
    k = lax.shift_right_logical(j, 5)
    off = (k * STRIDE) & (PEERS - 1)
    x = (me + off) & 3
    y = (lax.shift_right_logical(off, 2) + me // SIDE) & 3
    z = (lax.shift_right_logical(off, 4) + me // (SIDE * SIDE)) & 3
    return (z * 16 + y * 4 + x) * CAP + (j & (CAP - 1))


def kernel(
    routes, samples, cotangent, weights, one, two,
    outputs, new_w, new_one, new_two,
    sv, cv, wf, m1, m2, wh, wl, sp, cp, arr, arc, ret, ah, al, slope, grads, got, slot, slot_t, o_w, o_1, o_2,
    in_sem, out_sem, send_sem, recv_sem, w_sem, g_sem,
):
    me = lax.axis_index("expert")
    rep = lax.axis_index("replica")
    other = 1 - rep

    loads = [
        pltpu.make_async_copy(src, dst, in_sem.at[i])
        for i, (src, dst) in enumerate(
            ((samples, sv), (weights, wf.at[rep]), (cotangent, cv), (one, m1), (two, m2))
        )
    ]
    for load in loads:
        load.start()

    barrier = pltpu.get_barrier_semaphore()

    def greet(k, carry):
        pl.semaphore_signal(barrier, inc=1, device_id={"expert": peer_back(me, k)}, device_id_type=MESH)
        return carry

    lax.fori_loop(1, PEERS, greet, 0)
    pl.semaphore_signal(barrier, inc=1, device_id={"replica": other}, device_id_type=MESH)

    route = routes[...]
    earlier = (
        lax.broadcasted_iota(jnp.int32, (256, 256), 0) < lax.broadcasted_iota(jnp.int32, (256, 256), 1)
    ).astype(F32).astype(BF16)
    experts = lax.broadcasted_iota(jnp.int32, (PEERS, 256), 0)
    base = jnp.zeros((PEERS, 1), F32)
    for b in range(ROWS // 256):
        part = route[:, b * 256 : (b + 1) * 256]
        hot = (experts == part).astype(F32)
        before = mm(hot.astype(BF16), earlier) + base
        rank = jnp.sum(hot * before, axis=0, keepdims=True)
        base = base + jnp.sum(hot, axis=1, keepdims=True)
        slot[:, b * 256 : (b + 1) * 256] = part * CAP + rank.astype(jnp.int32)

    def remote(phase, src, dst, k, g, to):
        return pltpu.make_async_remote_copy(
            src_ref=src, dst_ref=dst, send_sem=send_sem.at[phase], recv_sem=recv_sem.at[phase, g],
            device_id={"expert": to}, device_id_type=MESH,
        )

    def send_group(phase, src, dst, g, where):
        @pl.when(g == 0)
        def _():
            pltpu.make_async_copy(src.at[0], dst.at[0], recv_sem.at[phase, 0]).start()

        @pl.when(g > 0)
        def _():
            k = g * PER
            remote(phase, src.at[k], dst.at[k], k, g, where(me, k)).start()

        def one_send(i, carry):
            k = g * PER + i
            remote(phase, src.at[k], dst.at[k], k, g, where(me, k)).start()
            return carry

        lax.fori_loop(1, PER, one_send, 0)

    def wait_group(phase, dst, g):
        block = dst.at[pl.ds(g * PER, PER)]
        remote(phase, block, block, 0, g, me).wait_recv()

    def pack_group(high, low, dst, g):
        want = wanted(me, g, (TILE, 128), 0)
        want = jnp.concatenate([want] * (ROWS // 128), axis=1)
        hot = (want == slot[...]).astype(F32).astype(BF16)
        packed = mm(hot, high) + mm(hot, low)
        dst[pl.ds(g * PER, PER)] = packed.reshape(PER, CAP, WIDTH)

    loads[0].wait()
    s_high, s_low = split(sv[...])
    loads[1].wait()
    pl.semaphore_wait(barrier, PEERS)
    weight_copy = pltpu.make_async_remote_copy(
        src_ref=wf.at[rep], dst_ref=wf.at[rep], send_sem=w_sem.at[0], recv_sem=w_sem.at[1],
        device_id={"replica": other}, device_id_type=MESH,
    )
    weight_copy.start()

    def pack_samples(g, carry):
        pack_group(s_high, s_low, sp, g)
        send_group(0, sp, arr, g, peer)
        return carry

    lax.fori_loop(0, GROUPS, pack_samples, 0)

    loads[2].wait()
    c_high, c_low = split(cv[...])

    def pack_cotangent(g, carry):
        pack_group(c_high, c_low, cp, g)
        send_group(1, cp, arc, g, peer)
        return carry

    lax.fori_loop(0, GROUPS, pack_cotangent, 0)

    slot_t[...] = jnp.transpose(jnp.broadcast_to(slot[...], (128, ROWS)))

    weight_copy.wait()

    def split_weights(layer, carry):
        for half in range(2):
            high, low = split(wf[half, layer])
            wh[layer, half * HALF : (half + 1) * HALF] = high
            wl[layer, half * HALF : (half + 1) * HALF] = low
        grads[0, layer] = jnp.zeros((HALF, WIDTH), F32)
        grads[1, layer] = jnp.zeros((HALF, WIDTH), F32)
        return carry

    lax.fori_loop(0, LAYERS, split_weights, 0)

    def forward(g, carry):
        wait_group(0, arr, g)
        rows = pl.ds(g * TILE, TILE)
        hidden = arr[pl.ds(g * PER, PER)].reshape(TILE, WIDTH)
        for layer in range(LAYERS):
            high, low = split(hidden)
            ah[layer, rows] = high
            al[layer, rows] = low
            pre = mm(high, wh[layer]) + mm(low, wh[layer]) + mm(high, wl[layer])
            if layer < LAYERS - 1:
                sigma = jax.nn.sigmoid(pre)
                hidden = pre * sigma
                slope[layer, rows] = sigma * (1.0 + pre * (1.0 - sigma))
        arr[pl.ds(g * PER, PER)] = pre.reshape(PER, CAP, WIDTH)
        send_group(2, arr, ret, g, peer_back)
        return carry

    lax.fori_loop(0, GROUPS, forward, 0)

    def backward(g, carry):
        wait_group(1, arc, g)
        rows = pl.ds(g * TILE, TILE)
        delta = arc[pl.ds(g * PER, PER)].reshape(TILE, WIDTH)
        for layer in range(LAYERS - 1, -1, -1):
            high, low = split(delta)
            a_high, a_low = ah[layer, rows], al[layer, rows]
            grad = mm_tn(a_high, high) + mm_tn(a_high, low) + mm_tn(a_low, high)
            grads[0, layer] += grad[:HALF]
            grads[1, layer] += grad[HALF:]
            if layer > 0:
                back = mm_nt(high, wh[layer]) + mm_nt(low, wh[layer]) + mm_nt(high, wl[layer])
                delta = back * slope[layer - 1, rows]
        return carry

    lax.fori_loop(0, GROUPS, backward, 0)

    grad_copy = pltpu.make_async_remote_copy(
        src_ref=grads.at[other], dst_ref=got, send_sem=g_sem.at[0], recv_sem=g_sem.at[1],
        device_id={"replica": other}, device_id_type=MESH,
    )
    grad_copy.start()
    loads[3].wait()
    loads[4].wait()
    grad_copy.wait()

    def adam(layer, carry):
        grad = grads[rep, layer] + got[layer]
        first = 0.9 * m1[layer] + 0.1 * grad
        second = 0.999 * m2[layer] + 0.001 * grad * grad
        o_1[layer] = first
        o_2[layer] = second
        o_w[layer] = wf[rep, layer] - 0.01 * (first / CORR_ONE) / (jnp.sqrt(second / CORR_TWO) + 1e-08)
        return carry

    lax.fori_loop(0, LAYERS, adam, 0)
    stores = [
        pltpu.make_async_copy(src, dst, out_sem.at[i])
        for i, (src, dst) in enumerate(((o_w, new_w), (o_1, new_one), (o_2, new_two)))
    ]
    for store in stores:
        store.start()

    outputs[...] = jnp.zeros((ROWS, WIDTH), F32)

    def unpack(g, carry):
        wait_group(2, ret, g)
        high, low = split(ret[pl.ds(g * PER, PER)].reshape(TILE, WIDTH))
        want = wanted(me, g, (8, TILE), 1)[:1]

        def some_rows(i, carry):
            rows = pl.ds(i * 256, 256)
            mine = slot_t[rows]
            mine = jnp.concatenate([mine, mine], axis=1)
            hot = (mine == want).astype(F32).astype(BF16)
            outputs[rows] += mm(hot, high) + mm(hot, low)
            return carry

        lax.fori_loop(0, ROWS // 256, some_rows, 0)
        return carry

    lax.fori_loop(0, GROUPS, unpack, 0)

    for store in stores:
        store.wait()
    for phase, src in enumerate((sp, cp, arr)):
        block = src.at[pl.ds(1, PEERS - 1)]
        remote(phase, block, block, 0, 0, me).wait_send()


def on_device(samples, routes, cotangent, weights, moment_one, moment_two):
    shard = (LAYERS, HALF, WIDTH)
    state = jax.ShapeDtypeStruct(shard, F32)
    hbm = pl.BlockSpec(memory_space=pl.ANY)
    vmem = pl.BlockSpec(memory_space=pltpu.VMEM)
    peers = (PEERS, CAP, WIDTH)
    slots = PEERS * CAP
    flops = 2 * slots * WIDTH * WIDTH * 60
    outputs, new_w, new_one, new_two = pl.pallas_call(
        kernel,
        out_shape=(jax.ShapeDtypeStruct((ROWS, WIDTH), F32), state, state, state),
        in_specs=[vmem] + [hbm] * 5,
        out_specs=(vmem, hbm, hbm, hbm),
        scratch_shapes=[
            pltpu.VMEM((ROWS, WIDTH), F32),
            pltpu.VMEM((ROWS, WIDTH), F32),
            pltpu.VMEM((2,) + shard, F32),
            pltpu.VMEM(shard, F32),
            pltpu.VMEM(shard, F32),
            pltpu.VMEM((LAYERS, WIDTH, WIDTH), BF16),
            pltpu.VMEM((LAYERS, WIDTH, WIDTH), BF16),
            pltpu.VMEM(peers, F32),
            pltpu.VMEM(peers, F32),
            pltpu.VMEM(peers, F32),
            pltpu.VMEM(peers, F32),
            pltpu.VMEM(peers, F32),
            pltpu.VMEM((LAYERS, slots, WIDTH), BF16),
            pltpu.VMEM((LAYERS, slots, WIDTH), BF16),
            pltpu.VMEM((LAYERS - 1, slots, WIDTH), F32),
            pltpu.VMEM((2,) + shard, F32),
            pltpu.VMEM(shard, F32),
            pltpu.VMEM((1, ROWS), jnp.int32),
            pltpu.VMEM((ROWS, 128), jnp.int32),
            pltpu.VMEM(shard, F32),
            pltpu.VMEM(shard, F32),
            pltpu.VMEM(shard, F32),
            pltpu.SemaphoreType.DMA((5,)),
            pltpu.SemaphoreType.DMA((3,)),
            pltpu.SemaphoreType.DMA((3,)),
            pltpu.SemaphoreType.DMA((3, GROUPS)),
            pltpu.SemaphoreType.DMA((2,)),
            pltpu.SemaphoreType.DMA((2,)),
        ],
        compiler_params=pltpu.CompilerParams(
            collective_id=0, has_side_effects=True, vmem_limit_bytes=60 * 2**20
        ),
        cost_estimate=pl.CostEstimate(flops=flops, bytes_accessed=2**23, transcendentals=slots * WIDTH * 6),
    )(
        routes.reshape(1, ROWS),
        samples,
        cotangent,
        weights[:, 0],
        moment_one[:, 0],
        moment_two[:, 0],
    )
    return outputs, new_w[:, None], new_one[:, None], new_two[:, None]


def solution(mesh):
    rows = P(("expert", "replica"), None)
    state = P(None, "expert", "replica", None)
    return jax.shard_map(
        on_device,
        mesh=mesh,
        in_specs=(rows, rows, rows, state, state, state),
        out_specs=(rows, state, state, state),
        check_vma=False,
    )
```

```python
import jax
import jax.numpy as jnp
from jax import lax
from jax.experimental import pallas as pl
from jax.experimental.pallas import tpu as pltpu
from jax.sharding import PartitionSpec as P

MESH = pl.DeviceIdType.MESH
CORR_ONE = 0.9999734386011124
CORR_TWO = 0.09520785288629038
F32 = jnp.float32
BF16 = jnp.bfloat16

SIDE = 4
PEERS = SIDE**3
CAP = 32
WIDTH = 256
ROWS = 1024
LAYERS = 7
HALF = WIDTH // 2
PER = 16
GROUPS = PEERS // PER
TILE = PER * CAP
PACK = 8
PACKS = PEERS // PACK
PACK_TILE = PACK * CAP
STRIDE = 37


def split(value):
    high = value.astype(BF16)
    low = (value - high.astype(F32)).astype(BF16)
    return high, low


def mm(a, b):
    return lax.dot_general(a, b, (((1,), (0,)), ((), ())), preferred_element_type=F32)


def mm_nt(a, b):
    return lax.dot_general(a, b, (((1,), (1,)), ((), ())), preferred_element_type=F32)


def mm_tn(a, b):
    return lax.dot_general(a, b, (((0,), (0,)), ((), ())), preferred_element_type=F32)


def peer(me, k):
    off = (k * STRIDE) % PEERS
    x = (me + off) % SIDE
    y = (me // SIDE + off // SIDE) % SIDE
    z = (me // (SIDE * SIDE) + off // (SIDE * SIDE)) % SIDE
    return z * (SIDE * SIDE) + y * SIDE + x


def peer_back(me, k):
    off = (k * STRIDE) % PEERS
    x = (me + SIDE - off % SIDE) % SIDE
    y = (me // SIDE + SIDE - (off // SIDE) % SIDE) % SIDE
    z = (me // (SIDE * SIDE) + SIDE - off // (SIDE * SIDE)) % SIDE
    return z * (SIDE * SIDE) + y * SIDE + x


def wanted(me, start, shape, axis):
    j = lax.broadcasted_iota(jnp.int32, shape, axis) + start
    k = lax.shift_right_logical(j, 5)
    off = (k * STRIDE) & (PEERS - 1)
    x = (me + off) & 3
    y = (lax.shift_right_logical(off, 2) + me // SIDE) & 3
    z = (lax.shift_right_logical(off, 4) + me // (SIDE * SIDE)) & 3
    return (z * 16 + y * 4 + x) * CAP + (j & (CAP - 1))


def kernel(
    routes, samples, cotangent, weights, one, two,
    outputs, new_w, new_one, new_two,
    sv, cv, wf, m1, m2, wh, wl, sp, cp, arr, arc, ret, ah, al, slope, grads, got, slot, slot_t, place,
    in_sem, send_sem, recv_sem, w_sem, g_sem,
):
    me = lax.axis_index("expert")
    rep = lax.axis_index("replica")
    other = 1 - rep

    loads = [
        pltpu.make_async_copy(src, dst, in_sem.at[i])
        for i, (src, dst) in enumerate(
            ((samples, sv), (weights, wf.at[rep]), (cotangent, cv), (one, m1), (two, m2))
        )
    ]
    for load in loads:
        load.start()

    barrier = pltpu.get_barrier_semaphore()

    def greet(k, carry):
        pl.semaphore_signal(barrier, inc=1, device_id={"expert": peer_back(me, k)}, device_id_type=MESH)
        return carry

    lax.fori_loop(1, PEERS, greet, 0)
    pl.semaphore_signal(barrier, inc=1, device_id={"replica": other}, device_id_type=MESH)

    route = routes[...]
    earlier = (
        lax.broadcasted_iota(jnp.int32, (256, 256), 0) < lax.broadcasted_iota(jnp.int32, (256, 256), 1)
    ).astype(F32).astype(BF16)
    experts = lax.broadcasted_iota(jnp.int32, (PEERS, 256), 0)
    base = jnp.zeros((PEERS, 1), F32)
    for b in range(ROWS // 256):
        part = route[:, b * 256 : (b + 1) * 256]
        hot = (experts == part).astype(F32)
        before = mm(hot.astype(BF16), earlier) + base
        rank = jnp.sum(hot * before, axis=0, keepdims=True)
        base = base + jnp.sum(hot, axis=1, keepdims=True)
        slot[:, b * 256 : (b + 1) * 256] = part * CAP + rank.astype(jnp.int32)

    def remote(phase, src, dst, k, to):
        return pltpu.make_async_remote_copy(
            src_ref=src, dst_ref=dst, send_sem=send_sem.at[phase], recv_sem=recv_sem.at[phase, k // PER],
            device_id={"expert": to}, device_id_type=MESH,
        )

    def send_range(phase, src, dst, start, count, where):
        @pl.when(start == 0)
        def _():
            pltpu.make_async_copy(src.at[0], dst.at[0], recv_sem.at[phase, 0]).start()

        @pl.when(start > 0)
        def _():
            remote(phase, src.at[start], dst.at[start], start, where(me, start)).start()

        def one_send(i, carry):
            k = start + i
            remote(phase, src.at[k], dst.at[k], k, where(me, k)).start()
            return carry

        lax.fori_loop(1, count, one_send, 0)

    def wait_group(phase, dst, g):
        block = dst.at[pl.ds(g * PER, PER)]
        remote(phase, block, block, g * PER, me).wait_recv()

    def pack_group(high, low, dst, g):
        want = wanted(me, g * PACK_TILE, (PACK_TILE, 128), 0)
        want = jnp.concatenate([want] * (ROWS // 128), axis=1)
        hot = (want == slot[...]).astype(F32).astype(BF16)
        packed = mm(hot, high) + mm(hot, low)
        dst[pl.ds(g * PACK, PACK)] = packed.reshape(PACK, CAP, WIDTH)

    loads[0].wait()
    s_high, s_low = split(sv[...])
    loads[1].wait()
    pl.semaphore_wait(barrier, PEERS)
    weight_copy = pltpu.make_async_remote_copy(
        src_ref=wf.at[rep], dst_ref=wf.at[rep], send_sem=w_sem.at[0], recv_sem=w_sem.at[1],
        device_id={"replica": other}, device_id_type=MESH,
    )
    weight_copy.start()

    def pack_samples(g, carry):
        pack_group(s_high, s_low, sp, g)
        send_range(0, sp, arr, g * PACK, PACK, peer)
        return carry

    lax.fori_loop(0, PACKS, pack_samples, 0)

    loads[2].wait()
    c_high, c_low = split(cv[...])

    def pack_cotangent(g, carry):
        pack_group(c_high, c_low, cp, g)
        send_range(1, cp, arc, g * PACK, PACK, peer)
        return carry

    lax.fori_loop(0, PACKS, pack_cotangent, 0)

    slot_t[...] = jnp.transpose(jnp.broadcast_to(slot[...], (128, ROWS)))

    def spread_rows(g, carry):
        want = wanted(me, g * TILE, (8, TILE), 1)[:1]

        def some_rows(i, carry):
            rows = pl.ds(i * 256, 256)
            mine = jnp.concatenate([slot_t[rows]] * (TILE // 128), axis=1)
            place[g, rows] = (mine == want).astype(F32).astype(BF16)
            return carry

        return lax.fori_loop(0, ROWS // 256, some_rows, carry)

    lax.fori_loop(0, GROUPS, spread_rows, 0)

    weight_copy.wait()

    def split_weights(layer, carry):
        for half in range(2):
            high, low = split(wf[half, layer])
            wh[layer, half * HALF : (half + 1) * HALF] = high
            wl[layer, half * HALF : (half + 1) * HALF] = low
        grads[0, layer] = jnp.zeros((HALF, WIDTH), F32)
        grads[1, layer] = jnp.zeros((HALF, WIDTH), F32)
        return carry

    lax.fori_loop(0, LAYERS, split_weights, 0)

    def forward(g, carry):
        wait_group(0, arr, g)
        rows = pl.ds(g * TILE, TILE)
        hidden = arr[pl.ds(g * PER, PER)].reshape(TILE, WIDTH)
        for layer in range(LAYERS):
            high, low = split(hidden)
            ah[layer, rows] = high
            al[layer, rows] = low
            pre = mm(high, wh[layer]) + mm(low, wh[layer]) + mm(high, wl[layer])
            if layer < LAYERS - 1:
                sigma = jax.nn.sigmoid(pre)
                hidden = pre * sigma
                slope[layer, rows] = sigma + hidden * (1.0 - sigma)
        arr[pl.ds(g * PER, PER)] = pre.reshape(PER, CAP, WIDTH)
        return carry

    lax.fori_loop(0, GROUPS, forward, 0)

    def backward(g, carry):
        send_range(2, arr, ret, g * PER, PER, peer_back)
        wait_group(1, arc, g)
        rows = pl.ds(g * TILE, TILE)
        delta = arc[pl.ds(g * PER, PER)].reshape(TILE, WIDTH)
        for layer in range(LAYERS - 1, -1, -1):
            high, low = split(delta)
            a_high, a_low = ah[layer, rows], al[layer, rows]
            grad = mm_tn(a_high, high) + mm_tn(a_high, low) + mm_tn(a_low, high)
            grads[0, layer] += grad[:HALF]
            grads[1, layer] += grad[HALF:]
            if layer > 0:
                back = mm_nt(high, wh[layer]) + mm_nt(low, wh[layer]) + mm_nt(high, wl[layer])
                delta = back * slope[layer - 1, rows]
        return carry

    def unpack(g, first):
        wait_group(2, ret, g)
        high, low = split(ret[pl.ds(g * PER, PER)].reshape(TILE, WIDTH))

        def some_rows(i, carry):
            rows = pl.ds(i * 256, 256)
            hot = place[g, rows]
            found = mm(hot, high) + mm(hot, low)
            outputs[rows] = found if first else outputs[rows] + found
            return carry

        lax.fori_loop(0, ROWS // 256, some_rows, 0)

    lax.fori_loop(0, GROUPS - 1, backward, 0)
    unpack(0, True)
    backward(GROUPS - 1, 0)

    grad_copy = pltpu.make_async_remote_copy(
        src_ref=grads.at[other], dst_ref=got, send_sem=g_sem.at[0], recv_sem=g_sem.at[1],
        device_id={"replica": other}, device_id_type=MESH,
    )
    grad_copy.start()
    unpack(1, False)
    loads[3].wait()
    loads[4].wait()
    grad_copy.wait()

    def adam(layer, carry):
        grad = grads[rep, layer] + got[layer]
        first = 0.9 * m1[layer] + 0.1 * grad
        second = 0.999 * m2[layer] + 0.001 * grad * grad
        new_one[layer] = first
        new_two[layer] = second
        new_w[layer] = wf[rep, layer] - 0.01 * (first / CORR_ONE) / (jnp.sqrt(second / CORR_TWO) + 1e-08)
        return carry

    lax.fori_loop(0, LAYERS, adam, 0)
    for g in range(2, GROUPS):
        unpack(g, False)

    for phase, src in enumerate((sp, cp, arr)):
        block = src.at[pl.ds(1, PEERS - 1)]
        remote(phase, block, block, 0, me).wait_send()


def store_kernel(a, b, c, d, out_a, out_b, out_c, out_d, sem):
    copies = [
        pltpu.make_async_copy(src, dst, sem.at[i])
        for i, (src, dst) in enumerate(((a, out_a), (b, out_b), (c, out_c), (d, out_d)))
    ]
    for copy in copies:
        copy.start()
    for copy in copies:
        copy.wait()


def on_device(samples, routes, cotangent, weights, moment_one, moment_two):
    shard = (LAYERS, HALF, WIDTH)
    state = jax.ShapeDtypeStruct(shard, F32)
    hbm = pl.BlockSpec(memory_space=pl.ANY)
    vmem = pl.BlockSpec(memory_space=pltpu.VMEM)
    peers = (PEERS, CAP, WIDTH)
    slots = PEERS * CAP
    flops = 2 * slots * WIDTH * WIDTH * 60
    held = pl.pallas_call(
        kernel,
        out_shape=(pltpu.VMEM((ROWS, WIDTH), F32),) + (pltpu.VMEM(shard, F32),) * 3,
        in_specs=[vmem] + [hbm] * 5,
        out_specs=(vmem,) * 4,
        scratch_shapes=[
            pltpu.VMEM((ROWS, WIDTH), F32),
            pltpu.VMEM((ROWS, WIDTH), F32),
            pltpu.VMEM((2,) + shard, F32),
            pltpu.VMEM(shard, F32),
            pltpu.VMEM(shard, F32),
            pltpu.VMEM((LAYERS, WIDTH, WIDTH), BF16),
            pltpu.VMEM((LAYERS, WIDTH, WIDTH), BF16),
            pltpu.VMEM(peers, F32),
            pltpu.VMEM(peers, F32),
            pltpu.VMEM(peers, F32),
            pltpu.VMEM(peers, F32),
            pltpu.VMEM(peers, F32),
            pltpu.VMEM((LAYERS, slots, WIDTH), BF16),
            pltpu.VMEM((LAYERS, slots, WIDTH), BF16),
            pltpu.VMEM((LAYERS - 1, slots, WIDTH), F32),
            pltpu.VMEM((2,) + shard, F32),
            pltpu.VMEM(shard, F32),
            pltpu.VMEM((1, ROWS), jnp.int32),
            pltpu.VMEM((ROWS, 128), jnp.int32),
            pltpu.VMEM((GROUPS, ROWS, TILE), BF16),
            pltpu.SemaphoreType.DMA((5,)),
            pltpu.SemaphoreType.DMA((3,)),
            pltpu.SemaphoreType.DMA((3, GROUPS)),
            pltpu.SemaphoreType.DMA((2,)),
            pltpu.SemaphoreType.DMA((2,)),
        ],
        compiler_params=pltpu.CompilerParams(
            collective_id=0, has_side_effects=True, vmem_limit_bytes=56 * 2**20
        ),
        cost_estimate=pl.CostEstimate(flops=flops, bytes_accessed=2**23, transcendentals=slots * WIDTH * 6),
    )(
        routes.reshape(1, ROWS),
        samples,
        cotangent,
        weights[:, 0],
        moment_one[:, 0],
        moment_two[:, 0],
    )
    outputs, new_w, new_one, new_two = pl.pallas_call(
        store_kernel,
        out_shape=(jax.ShapeDtypeStruct((ROWS, WIDTH), F32), state, state, state),
        in_specs=[vmem] * 4,
        out_specs=(hbm,) * 4,
        scratch_shapes=[pltpu.SemaphoreType.DMA((4,))],
        compiler_params=pltpu.CompilerParams(vmem_limit_bytes=2**22),
    )(*(pltpu.with_memory_space_constraint(x, pltpu.VMEM) for x in held))
    return outputs, new_w[:, None], new_one[:, None], new_two[:, None]


def solution(mesh):
    rows = P(("expert", "replica"), None)
    state = P(None, "expert", "replica", None)
    return jax.shard_map(
        on_device,
        mesh=mesh,
        in_specs=(rows, rows, rows, state, state, state),
        out_specs=(rows, state, state, state),
        check_vma=False,
    )
```

```python
import jax
import jax.numpy as jnp
from jax import lax
from jax.experimental import pallas as pl
from jax.experimental.pallas import tpu as pltpu
from jax.sharding import PartitionSpec as P

MESH = pl.DeviceIdType.MESH
CORR_ONE = 0.9999734386011124
CORR_TWO = 0.09520785288629038
F32 = jnp.float32
BF16 = jnp.bfloat16

SIDE = 4
PEERS = SIDE**3
CAP = 32
WIDTH = 256
ROWS = 1024
LAYERS = 7
HALF = WIDTH // 2
PER = 16
GROUPS = PEERS // PER
TILE = PER * CAP
PACK = 8
PACKS = PEERS // PACK
PACK_TILE = PACK * CAP
STRIDE = 27


def split(value):
    high = value.astype(BF16)
    low = (value - high.astype(F32)).astype(BF16)
    return high, low


def mm(a, b):
    return lax.dot_general(a, b, (((1,), (0,)), ((), ())), preferred_element_type=F32)


def mm_nt(a, b):
    return lax.dot_general(a, b, (((1,), (1,)), ((), ())), preferred_element_type=F32)


def mm_tn(a, b):
    return lax.dot_general(a, b, (((0,), (0,)), ((), ())), preferred_element_type=F32)


def peer(me, k):
    off = lax.rem(k * STRIDE, PEERS)
    x = lax.rem(me + off, SIDE)
    y = lax.rem(lax.div(me, SIDE) + lax.div(off, SIDE), SIDE)
    z = lax.rem(lax.div(me, SIDE * SIDE) + lax.div(off, SIDE * SIDE), SIDE)
    return z * (SIDE * SIDE) + y * SIDE + x


def peer_back(me, k):
    off = lax.rem(k * STRIDE, PEERS)
    x = lax.rem(me + SIDE - lax.rem(off, SIDE), SIDE)
    y = lax.rem(lax.div(me, SIDE) + SIDE - lax.rem(lax.div(off, SIDE), SIDE), SIDE)
    z = lax.rem(lax.div(me, SIDE * SIDE) + SIDE - lax.div(off, SIDE * SIDE), SIDE)
    return z * (SIDE * SIDE) + y * SIDE + x


def wanted(me, start, shape, axis):
    j = lax.broadcasted_iota(jnp.int32, shape, axis) + start
    k = lax.shift_right_logical(j, 5)
    off = (k * STRIDE) & (PEERS - 1)
    x = (me + off) & 3
    y = (lax.shift_right_logical(off, 2) + me // SIDE) & 3
    z = (lax.shift_right_logical(off, 4) + me // (SIDE * SIDE)) & 3
    return (z * 16 + y * 4 + x) * CAP + (j & (CAP - 1))


def kernel(
    routes, samples, cotangent, weights, one, two,
    ret, place, outputs, new_w, new_one, new_two,
    sv, cv, wf, m1, m2, wh, wl, sp, cp, arr, arc, ah, al, slope, grads, got, slot, slot_t,
    in_sem, send_sem, recv_sem, w_sem, g_sem,
):
    me = lax.axis_index("expert")
    rep = lax.axis_index("replica")
    other = 1 - rep

    barrier = pltpu.get_barrier_semaphore()
    at_x = lax.rem(me, SIDE)
    at_y = lax.rem(lax.div(me, SIDE), SIDE)
    at_z = lax.div(me, SIDE * SIDE)
    xs, ys, zs = (
        [at] + [lax.rem(at + step, SIDE) for step in range(1, SIDE)] for at in (at_x, at_y, at_z)
    )
    for off in range(PEERS - 1, 0, -1):
        z, y, x = zs[off // 16], ys[off // 4 % 4], xs[off % 4]
        to = z * (SIDE * SIDE) + y * SIDE + x
        pl.semaphore_signal(barrier, inc=1, device_id={"expert": to}, device_id_type=MESH)
    pl.semaphore_signal(barrier, inc=1, device_id={"replica": other}, device_id_type=MESH)

    loads = [
        pltpu.make_async_copy(src, dst, in_sem.at[i])
        for i, (src, dst) in enumerate(
            ((samples, sv), (weights, wf.at[rep]), (cotangent, cv), (one, m1), (two, m2))
        )
    ]
    for load in loads:
        load.start()

    route = routes[...]
    earlier = (
        lax.broadcasted_iota(jnp.int32, (256, 256), 0) < lax.broadcasted_iota(jnp.int32, (256, 256), 1)
    ).astype(F32).astype(BF16)
    experts = lax.broadcasted_iota(jnp.int32, (PEERS, 256), 0)
    base = jnp.zeros((PEERS, 1), F32)
    for b in range(ROWS // 256):
        part = route[:, b * 256 : (b + 1) * 256]
        hot = (experts == part).astype(F32)
        before = mm(hot.astype(BF16), earlier) + base
        rank = jnp.sum(hot * before, axis=0, keepdims=True)
        base = base + jnp.sum(hot, axis=1, keepdims=True)
        slot[:, b * 256 : (b + 1) * 256] = part * CAP + rank.astype(jnp.int32)

    def remote(phase, src, dst, k, to):
        return pltpu.make_async_remote_copy(
            src_ref=src, dst_ref=dst, send_sem=send_sem.at[phase], recv_sem=recv_sem.at[phase, k // PER],
            device_id={"expert": to}, device_id_type=MESH,
        )

    def send_range(phase, src, dst, start, count, where):
        @pl.when(start == 0)
        def _():
            pltpu.make_async_copy(src.at[0], dst.at[0], recv_sem.at[phase, 0]).start()

        @pl.when(start > 0)
        def _():
            remote(phase, src.at[start], dst.at[start], start, where(me, start)).start()

        def one_send(i, carry):
            k = start + i
            remote(phase, src.at[k], dst.at[k], k, where(me, k)).start()
            return carry

        lax.fori_loop(1, count, one_send, 0)

    def wait_group(phase, dst, g):
        block = dst.at[pl.ds(g * PER, PER)]
        remote(phase, block, block, g * PER, me).wait_recv()

    def pack_group(high, low, dst, g):
        want = wanted(me, g * PACK_TILE, (PACK_TILE, 128), 0)
        want = jnp.concatenate([want] * (ROWS // 128), axis=1)
        hot = (want == slot[...]).astype(F32).astype(BF16)
        packed = mm(hot, high) + mm(hot, low)
        dst[pl.ds(g * PACK, PACK)] = packed.reshape(PACK, CAP, WIDTH)

    loads[0].wait()
    s_high, s_low = split(sv[...])
    pack_group(s_high, s_low, sp, 0)
    pl.semaphore_wait(barrier, PEERS)
    send_range(0, sp, arr, 0, PACK, peer)
    loads[1].wait()
    weight_copy = pltpu.make_async_remote_copy(
        src_ref=wf.at[rep], dst_ref=wf.at[rep], send_sem=w_sem.at[0], recv_sem=w_sem.at[1],
        device_id={"replica": other}, device_id_type=MESH,
    )
    weight_copy.start()

    def pack_samples(g, carry):
        pack_group(s_high, s_low, sp, g)
        send_range(0, sp, arr, g * PACK, PACK, peer)
        return carry

    lax.fori_loop(1, PACKS, pack_samples, 0)

    loads[2].wait()
    c_high, c_low = split(cv[...])

    def pack_cotangent(g, carry):
        pack_group(c_high, c_low, cp, g)
        send_range(1, cp, arc, g * PACK, PACK, peer)
        return carry

    lax.fori_loop(0, PACKS, pack_cotangent, 0)

    slot_t[...] = jnp.transpose(jnp.broadcast_to(slot[...], (128, ROWS)))

    def spread_rows(g, carry):
        want = wanted(me, g * TILE, (8, TILE), 1)[:1]

        def some_rows(i, carry):
            rows = pl.ds(i * 256, 256)
            mine = jnp.concatenate([slot_t[rows]] * (TILE // 128), axis=1)
            place[g, rows] = (mine == want).astype(F32).astype(BF16)
            return carry

        return lax.fori_loop(0, ROWS // 256, some_rows, carry)

    lax.fori_loop(0, GROUPS, spread_rows, 0)

    weight_copy.wait()

    def split_weights(layer, carry):
        for half in range(2):
            high, low = split(wf[half, layer])
            wh[layer, half * HALF : (half + 1) * HALF] = high
            wl[layer, half * HALF : (half + 1) * HALF] = low
        grads[0, layer] = jnp.zeros((HALF, WIDTH), F32)
        grads[1, layer] = jnp.zeros((HALF, WIDTH), F32)
        return carry

    lax.fori_loop(0, LAYERS, split_weights, 0)

    def forward(g, carry):
        wait_group(0, arr, g)
        rows = pl.ds(g * TILE, TILE)
        hidden = arr[pl.ds(g * PER, PER)].reshape(TILE, WIDTH)
        for layer in range(LAYERS):
            high, low = split(hidden)
            ah[layer, rows] = high
            al[layer, rows] = low
            pre = mm(high, wh[layer]) + mm(low, wh[layer]) + mm(high, wl[layer])
            if layer < LAYERS - 1:
                sigma = jax.nn.sigmoid(pre)
                hidden = pre * sigma
                slope[layer, rows] = sigma + hidden * (1.0 - sigma)
        arr[pl.ds(g * PER, PER)] = pre.reshape(PER, CAP, WIDTH)
        return carry

    lax.fori_loop(0, GROUPS, forward, 0)

    def backward(g, carry):
        send_range(2, arr, ret, g * PER, PER, peer_back)
        wait_group(1, arc, g)
        rows = pl.ds(g * TILE, TILE)
        delta = arc[pl.ds(g * PER, PER)].reshape(TILE, WIDTH)
        for layer in range(LAYERS - 1, -1, -1):
            high, low = split(delta)
            a_high, a_low = ah[layer, rows], al[layer, rows]
            grad = mm_tn(a_high, high) + mm_tn(a_high, low) + mm_tn(a_low, high)
            grads[0, layer] += grad[:HALF]
            grads[1, layer] += grad[HALF:]
            if layer > 0:
                back = mm_nt(high, wh[layer]) + mm_nt(low, wh[layer]) + mm_nt(high, wl[layer])
                delta = back * slope[layer - 1, rows]
        return carry

    def unpack(g, first):
        wait_group(2, ret, g)
        high, low = split(ret[pl.ds(g * PER, PER)].reshape(TILE, WIDTH))

        def some_rows(i, carry):
            rows = pl.ds(i * 256, 256)
            hot = place[g, rows]
            found = mm(hot, high) + mm(hot, low)
            outputs[rows] = found if first else outputs[rows] + found
            return carry

        lax.fori_loop(0, ROWS // 256, some_rows, 0)

    lax.fori_loop(0, GROUPS - 1, backward, 0)
    unpack(0, True)
    backward(GROUPS - 1, 0)

    grad_copy = pltpu.make_async_remote_copy(
        src_ref=grads.at[other], dst_ref=got, send_sem=g_sem.at[0], recv_sem=g_sem.at[1],
        device_id={"replica": other}, device_id_type=MESH,
    )
    grad_copy.start()
    unpack(1, False)
    loads[3].wait()
    loads[4].wait()
    grad_copy.wait()

    def adam(layer, carry):
        grad = grads[rep, layer] + got[layer]
        first = 0.9 * m1[layer] + 0.1 * grad
        second = 0.999 * m2[layer] + 0.001 * grad * grad
        new_one[layer] = first
        new_two[layer] = second
        new_w[layer] = wf[rep, layer] - 0.01 * (first / CORR_ONE) / (jnp.sqrt(second / CORR_TWO) + 1e-08)
        return carry

    lax.fori_loop(0, LAYERS, adam, 0)
    for g in range(2, GROUPS - 1):
        unpack(g, False)
    wait_group(2, ret, GROUPS - 1)

    for phase, src in enumerate((sp, cp, arr)):
        block = src.at[pl.ds(1, PEERS - 1)]
        remote(phase, block, block, 0, me).wait_send()


def finish(ret, place, partial, w, one, two, outputs, new_w, new_one, new_two, rows_out, sem):
    copies = [
        pltpu.make_async_copy(src, dst, sem.at[i])
        for i, (src, dst) in enumerate(((w, new_w), (one, new_one), (two, new_two)))
    ]
    for copy in copies:
        copy.start()
    high, low = split(ret[PEERS - PER :].reshape(TILE, WIDTH))
    part = 256
    for i in range(ROWS // part):
        rows = pl.ds(i * part, part)
        hot = place[GROUPS - 1, rows]
        rows_out[rows] = partial[rows] + mm(hot, high) + mm(hot, low)
        copies.append(pltpu.make_async_copy(rows_out.at[rows], outputs.at[rows], sem.at[3 + i]))
        copies[-1].start()
    for copy in copies:
        copy.wait()


def on_device(samples, routes, cotangent, weights, moment_one, moment_two):
    shard = (LAYERS, HALF, WIDTH)
    state = jax.ShapeDtypeStruct(shard, F32)
    hbm = pl.BlockSpec(memory_space=pl.ANY)
    vmem = pl.BlockSpec(memory_space=pltpu.VMEM)
    peers = (PEERS, CAP, WIDTH)
    slots = PEERS * CAP
    flops = 2 * slots * WIDTH * WIDTH * 60
    held = pl.pallas_call(
        kernel,
        out_shape=(
            pltpu.VMEM(peers, F32),
            pltpu.VMEM((GROUPS, ROWS, TILE), BF16),
            pltpu.VMEM((ROWS, WIDTH), F32),
            pltpu.VMEM(shard, F32),
            pltpu.VMEM(shard, F32),
            pltpu.VMEM(shard, F32),
        ),
        in_specs=[vmem] + [hbm] * 5,
        out_specs=(vmem,) * 6,
        scratch_shapes=[
            pltpu.VMEM((ROWS, WIDTH), F32),
            pltpu.VMEM((ROWS, WIDTH), F32),
            pltpu.VMEM((2,) + shard, F32),
            pltpu.VMEM(shard, F32),
            pltpu.VMEM(shard, F32),
            pltpu.VMEM((LAYERS, WIDTH, WIDTH), BF16),
            pltpu.VMEM((LAYERS, WIDTH, WIDTH), BF16),
            pltpu.VMEM(peers, F32),
            pltpu.VMEM(peers, F32),
            pltpu.VMEM(peers, F32),
            pltpu.VMEM(peers, F32),
            pltpu.VMEM((LAYERS, slots, WIDTH), BF16),
            pltpu.VMEM((LAYERS, slots, WIDTH), BF16),
            pltpu.VMEM((LAYERS - 1, slots, WIDTH), F32),
            pltpu.VMEM((2,) + shard, F32),
            pltpu.VMEM(shard, F32),
            pltpu.VMEM((1, ROWS), jnp.int32),
            pltpu.VMEM((ROWS, 128), jnp.int32),
            pltpu.SemaphoreType.DMA((5,)),
            pltpu.SemaphoreType.DMA((3,)),
            pltpu.SemaphoreType.DMA((3, GROUPS)),
            pltpu.SemaphoreType.DMA((2,)),
            pltpu.SemaphoreType.DMA((2,)),
        ],
        compiler_params=pltpu.CompilerParams(
            collective_id=0, has_side_effects=True, vmem_limit_bytes=50 * 2**20
        ),
        cost_estimate=pl.CostEstimate(flops=flops, bytes_accessed=2**23, transcendentals=slots * WIDTH * 6),
    )(
        routes.reshape(1, ROWS),
        samples,
        cotangent,
        weights[:, 0],
        moment_one[:, 0],
        moment_two[:, 0],
    )
    outputs, new_w, new_one, new_two = pl.pallas_call(
        finish,
        out_shape=(jax.ShapeDtypeStruct((ROWS, WIDTH), F32), state, state, state),
        in_specs=[vmem] * 6,
        out_specs=(hbm,) * 4,
        scratch_shapes=[pltpu.VMEM((ROWS, WIDTH), F32), pltpu.SemaphoreType.DMA((7,))],
        compiler_params=pltpu.CompilerParams(vmem_limit_bytes=2**23),
    )(*(pltpu.with_memory_space_constraint(x, pltpu.VMEM) for x in held))
    return outputs, new_w[:, None], new_one[:, None], new_two[:, None]


def solution(mesh):
    rows = P(("expert", "replica"), None)
    state = P(None, "expert", "replica", None)
    return jax.shard_map(
        on_device,
        mesh=mesh,
        in_specs=(rows, rows, rows, state, state, state),
        out_specs=(rows, state, state, state),
        check_vma=False,
    )
```

```python
import jax
import jax.numpy as jnp
from jax import lax
from jax.experimental import pallas as pl
from jax.experimental.pallas import tpu as pltpu
from jax.sharding import PartitionSpec as P

MESH = pl.DeviceIdType.MESH
CORR_ONE = 0.9999734386011124
CORR_TWO = 0.09520785288629038
F32 = jnp.float32
BF16 = jnp.bfloat16

SIDE = 4
PEERS = SIDE**3
CAP = 32
WIDTH = 256
ROWS = 1024
LAYERS = 7
HALF = WIDTH // 2
PER = 16
GROUPS = PEERS // PER
TILE = PER * CAP
PACK = 8
PACKS = PEERS // PACK
PACK_TILE = PACK * CAP
STRIDE = 27


def split(value):
    high = value.astype(BF16)
    low = (value - high.astype(F32)).astype(BF16)
    return high, low


def mm(a, b):
    return lax.dot_general(a, b, (((1,), (0,)), ((), ())), preferred_element_type=F32)


def mm_nt(a, b):
    return lax.dot_general(a, b, (((1,), (1,)), ((), ())), preferred_element_type=F32)


def mm_tn(a, b):
    return lax.dot_general(a, b, (((0,), (0,)), ((), ())), preferred_element_type=F32)


def peer(me, k):
    off = lax.rem(k * STRIDE, PEERS)
    x = lax.rem(me + off, SIDE)
    y = lax.rem(lax.div(me, SIDE) + lax.div(off, SIDE), SIDE)
    z = lax.rem(lax.div(me, SIDE * SIDE) + lax.div(off, SIDE * SIDE), SIDE)
    return z * (SIDE * SIDE) + y * SIDE + x


def peer_back(me, k):
    off = lax.rem(k * STRIDE, PEERS)
    x = lax.rem(me + SIDE - lax.rem(off, SIDE), SIDE)
    y = lax.rem(lax.div(me, SIDE) + SIDE - lax.rem(lax.div(off, SIDE), SIDE), SIDE)
    z = lax.rem(lax.div(me, SIDE * SIDE) + SIDE - lax.div(off, SIDE * SIDE), SIDE)
    return z * (SIDE * SIDE) + y * SIDE + x


def wanted(me, start, shape, axis):
    j = lax.broadcasted_iota(jnp.int32, shape, axis) + start
    k = lax.shift_right_logical(j, 5)
    off = (k * STRIDE) & (PEERS - 1)
    x = (me + off) & 3
    y = (lax.shift_right_logical(off, 2) + me // SIDE) & 3
    z = (lax.shift_right_logical(off, 4) + me // (SIDE * SIDE)) & 3
    return (z * 16 + y * 4 + x) * CAP + (j & (CAP - 1))


def kernel(
    routes, samples, cotangent, weights, one, two,
    ret, place, outputs, new_w, new_one, new_two,
    rv, sv, cv, wf, m1, m2, wh, wl, sp, cp, arr, arc, ah, al, slope, grads, got, slot, slot_t,
    in_sem, send_sem, recv_sem, w_sem, g_sem,
):
    me = lax.axis_index("expert")
    rep = lax.axis_index("replica")
    other = 1 - rep

    loads = [
        pltpu.make_async_copy(src, dst, in_sem.at[i])
        for i, (src, dst) in enumerate(
            ((samples, sv), (weights, wf.at[rep]), (cotangent, cv), (one, m1), (two, m2), (routes, rv))
        )
    ]
    loads[5].start()
    loads[0].start()

    barrier = pltpu.get_barrier_semaphore()
    at_x = lax.rem(me, SIDE)
    at_y = lax.rem(lax.div(me, SIDE), SIDE)
    at_z = lax.div(me, SIDE * SIDE)
    xs, ys, zs = (
        [at] + [lax.rem(at + step, SIDE) for step in range(1, SIDE)] for at in (at_x, at_y, at_z)
    )
    for off in range(PEERS - 1, 0, -1):
        z, y, x = zs[off // 16], ys[off // 4 % 4], xs[off % 4]
        to = z * (SIDE * SIDE) + y * SIDE + x
        pl.semaphore_signal(barrier, inc=1, device_id={"expert": to}, device_id_type=MESH)
    pl.semaphore_signal(barrier, inc=1, device_id={"replica": other}, device_id_type=MESH)

    for load in loads[1:5]:
        load.start()

    loads[5].wait()
    route = rv[...]
    earlier = (
        lax.broadcasted_iota(jnp.int32, (256, 256), 0) < lax.broadcasted_iota(jnp.int32, (256, 256), 1)
    ).astype(F32).astype(BF16)
    experts = lax.broadcasted_iota(jnp.int32, (PEERS, 256), 0)
    base = jnp.zeros((PEERS, 1), F32)
    for b in range(ROWS // 256):
        part = route[:, b * 256 : (b + 1) * 256]
        hot = (experts == part).astype(F32)
        before = mm(hot.astype(BF16), earlier) + base
        rank = jnp.sum(hot * before, axis=0, keepdims=True)
        base = base + jnp.sum(hot, axis=1, keepdims=True)
        slot[:, b * 256 : (b + 1) * 256] = part * CAP + rank.astype(jnp.int32)

    def remote(phase, src, dst, k, to):
        return pltpu.make_async_remote_copy(
            src_ref=src, dst_ref=dst, send_sem=send_sem.at[phase], recv_sem=recv_sem.at[phase, k // PER],
            device_id={"expert": to}, device_id_type=MESH,
        )

    def send_range(phase, src, dst, start, count, where):
        @pl.when(start == 0)
        def _():
            pltpu.make_async_copy(src.at[0], dst.at[0], recv_sem.at[phase, 0]).start()

        @pl.when(start > 0)
        def _():
            remote(phase, src.at[start], dst.at[start], start, where(me, start)).start()

        def one_send(i, carry):
            k = start + i
            remote(phase, src.at[k], dst.at[k], k, where(me, k)).start()
            return carry

        lax.fori_loop(1, count, one_send, 0)

    def wait_group(phase, dst, g):
        block = dst.at[pl.ds(g * PER, PER)]
        remote(phase, block, block, g * PER, me).wait_recv()

    def pack_group(high, low, dst, g):
        want = wanted(me, g * PACK_TILE, (PACK_TILE, 128), 0)
        want = jnp.concatenate([want] * (ROWS // 128), axis=1)
        hot = (want == slot[...]).astype(F32).astype(BF16)
        packed = mm(hot, high) + mm(hot, low)
        dst[pl.ds(g * PACK, PACK)] = packed.reshape(PACK, CAP, WIDTH)

    loads[0].wait()
    s_high, s_low = split(sv[...])
    pack_group(s_high, s_low, sp, 0)
    pl.semaphore_wait(barrier, PEERS)
    send_range(0, sp, arr, 0, PACK, peer)
    loads[1].wait()
    weight_copy = pltpu.make_async_remote_copy(
        src_ref=wf.at[rep], dst_ref=wf.at[rep], send_sem=w_sem.at[0], recv_sem=w_sem.at[1],
        device_id={"replica": other}, device_id_type=MESH,
    )
    weight_copy.start()

    def pack_samples(g, carry):
        pack_group(s_high, s_low, sp, g)
        send_range(0, sp, arr, g * PACK, PACK, peer)
        return carry

    lax.fori_loop(1, PACKS, pack_samples, 0)

    loads[2].wait()
    c_high, c_low = split(cv[...])

    def pack_cotangent(g, carry):
        pack_group(c_high, c_low, cp, g)
        send_range(1, cp, arc, g * PACK, PACK, peer)
        return carry

    lax.fori_loop(0, PACKS, pack_cotangent, 0)

    slot_t[...] = jnp.transpose(jnp.broadcast_to(slot[...], (128, ROWS)))

    def spread_rows(g, carry):
        want = wanted(me, g * TILE, (8, TILE), 1)[:1]

        def some_rows(i, carry):
            rows = pl.ds(i * 256, 256)
            mine = jnp.concatenate([slot_t[rows]] * (TILE // 128), axis=1)
            place[g, rows] = (mine == want).astype(F32).astype(BF16)
            return carry

        return lax.fori_loop(0, ROWS // 256, some_rows, carry)

    lax.fori_loop(0, GROUPS, spread_rows, 0)

    weight_copy.wait()

    def split_weights(layer, carry):
        for half in range(2):
            high, low = split(wf[half, layer])
            wh[layer, half * HALF : (half + 1) * HALF] = high
            wl[layer, half * HALF : (half + 1) * HALF] = low
        grads[0, layer] = jnp.zeros((HALF, WIDTH), F32)
        grads[1, layer] = jnp.zeros((HALF, WIDTH), F32)
        return carry

    lax.fori_loop(0, LAYERS, split_weights, 0)

    def forward(g, carry):
        wait_group(0, arr, g)
        rows = pl.ds(g * TILE, TILE)
        hidden = arr[pl.ds(g * PER, PER)].reshape(TILE, WIDTH)
        for layer in range(LAYERS):
            high, low = split(hidden)
            ah[layer, rows] = high
            al[layer, rows] = low
            pre = mm(high, wh[layer]) + mm(low, wh[layer]) + mm(high, wl[layer])
            if layer < LAYERS - 1:
                sigma = jax.nn.sigmoid(pre)
                hidden = pre * sigma
                slope[layer, rows] = sigma + hidden * (1.0 - sigma)
        arr[pl.ds(g * PER, PER)] = pre.reshape(PER, CAP, WIDTH)
        return carry

    lax.fori_loop(0, GROUPS, forward, 0)

    def backward(g, carry):
        send_range(2, arr, ret, g * PER, PER, peer_back)
        wait_group(1, arc, g)
        rows = pl.ds(g * TILE, TILE)
        delta = arc[pl.ds(g * PER, PER)].reshape(TILE, WIDTH)
        for layer in range(LAYERS - 1, -1, -1):
            high, low = split(delta)
            a_high, a_low = ah[layer, rows], al[layer, rows]
            grad = mm_tn(a_high, high) + mm_tn(a_high, low) + mm_tn(a_low, high)
            grads[0, layer] += grad[:HALF]
            grads[1, layer] += grad[HALF:]
            if layer > 0:
                back = mm_nt(high, wh[layer]) + mm_nt(low, wh[layer]) + mm_nt(high, wl[layer])
                delta = back * slope[layer - 1, rows]
        return carry

    def unpack(g, first):
        wait_group(2, ret, g)
        high, low = split(ret[pl.ds(g * PER, PER)].reshape(TILE, WIDTH))

        def some_rows(i, carry):
            rows = pl.ds(i * 256, 256)
            hot = place[g, rows]
            found = mm(hot, high) + mm(hot, low)
            outputs[rows] = found if first else outputs[rows] + found
            return carry

        lax.fori_loop(0, ROWS // 256, some_rows, 0)

    lax.fori_loop(0, GROUPS - 1, backward, 0)
    unpack(0, True)
    backward(GROUPS - 1, 0)

    grad_copy = pltpu.make_async_remote_copy(
        src_ref=grads.at[other], dst_ref=got, send_sem=g_sem.at[0], recv_sem=g_sem.at[1],
        device_id={"replica": other}, device_id_type=MESH,
    )
    grad_copy.start()
    unpack(1, False)
    loads[3].wait()
    loads[4].wait()
    grad_copy.wait()

    def adam(layer, carry):
        grad = grads[rep, layer] + got[layer]
        first = 0.9 * m1[layer] + 0.1 * grad
        second = 0.999 * m2[layer] + 0.001 * grad * grad
        new_one[layer] = first
        new_two[layer] = second
        new_w[layer] = wf[rep, layer] - 0.01 * (first / CORR_ONE) / (jnp.sqrt(second / CORR_TWO) + 1e-08)
        return carry

    lax.fori_loop(0, LAYERS, adam, 0)
    for g in range(2, GROUPS - 1):
        unpack(g, False)
    wait_group(2, ret, GROUPS - 1)

    for phase, src in enumerate((sp, cp, arr)):
        block = src.at[pl.ds(1, PEERS - 1)]
        remote(phase, block, block, 0, me).wait_send()


def finish(ret, place, partial, w, one, two, outputs, new_w, new_one, new_two, rows_out, sem):
    copies = [
        pltpu.make_async_copy(src, dst, sem.at[i])
        for i, (src, dst) in enumerate(((w, new_w), (one, new_one), (two, new_two)))
    ]
    for copy in copies:
        copy.start()
    high, low = split(ret[PEERS - PER :].reshape(TILE, WIDTH))
    part = 256
    for i in range(ROWS // part):
        rows = pl.ds(i * part, part)
        hot = place[GROUPS - 1, rows]
        rows_out[rows] = partial[rows] + mm(hot, high) + mm(hot, low)
        copies.append(pltpu.make_async_copy(rows_out.at[rows], outputs.at[rows], sem.at[3 + i]))
        copies[-1].start()
    for copy in copies:
        copy.wait()


def on_device(samples, routes, cotangent, weights, moment_one, moment_two):
    shard = (LAYERS, HALF, WIDTH)
    state = jax.ShapeDtypeStruct(shard, F32)
    hbm = pl.BlockSpec(memory_space=pl.ANY)
    vmem = pl.BlockSpec(memory_space=pltpu.VMEM)
    peers = (PEERS, CAP, WIDTH)
    slots = PEERS * CAP
    flops = 2 * slots * WIDTH * WIDTH * 60
    held = pl.pallas_call(
        kernel,
        out_shape=(
            pltpu.VMEM(peers, F32),
            pltpu.VMEM((GROUPS, ROWS, TILE), BF16),
            pltpu.VMEM((ROWS, WIDTH), F32),
            pltpu.VMEM(shard, F32),
            pltpu.VMEM(shard, F32),
            pltpu.VMEM(shard, F32),
        ),
        in_specs=[hbm] * 6,
        out_specs=(vmem,) * 6,
        scratch_shapes=[
            pltpu.VMEM((1, ROWS), jnp.int32),
            pltpu.VMEM((ROWS, WIDTH), F32),
            pltpu.VMEM((ROWS, WIDTH), F32),
            pltpu.VMEM((2,) + shard, F32),
            pltpu.VMEM(shard, F32),
            pltpu.VMEM(shard, F32),
            pltpu.VMEM((LAYERS, WIDTH, WIDTH), BF16),
            pltpu.VMEM((LAYERS, WIDTH, WIDTH), BF16),
            pltpu.VMEM(peers, F32),
            pltpu.VMEM(peers, F32),
            pltpu.VMEM(peers, F32),
            pltpu.VMEM(peers, F32),
            pltpu.VMEM((LAYERS, slots, WIDTH), BF16),
            pltpu.VMEM((LAYERS, slots, WIDTH), BF16),
            pltpu.VMEM((LAYERS - 1, slots, WIDTH), F32),
            pltpu.VMEM((2,) + shard, F32),
            pltpu.VMEM(shard, F32),
            pltpu.VMEM((1, ROWS), jnp.int32),
            pltpu.VMEM((ROWS, 128), jnp.int32),
            pltpu.SemaphoreType.DMA((6,)),
            pltpu.SemaphoreType.DMA((3,)),
            pltpu.SemaphoreType.DMA((3, GROUPS)),
            pltpu.SemaphoreType.DMA((2,)),
            pltpu.SemaphoreType.DMA((2,)),
        ],
        compiler_params=pltpu.CompilerParams(
            collective_id=0, has_side_effects=True, vmem_limit_bytes=50 * 2**20
        ),
        cost_estimate=pl.CostEstimate(flops=flops, bytes_accessed=2**23, transcendentals=slots * WIDTH * 6),
    )(
        routes.reshape(1, ROWS),
        samples,
        cotangent,
        weights[:, 0],
        moment_one[:, 0],
        moment_two[:, 0],
    )
    outputs, new_w, new_one, new_two = pl.pallas_call(
        finish,
        out_shape=(jax.ShapeDtypeStruct((ROWS, WIDTH), F32), state, state, state),
        in_specs=[vmem] * 6,
        out_specs=(hbm,) * 4,
        scratch_shapes=[pltpu.VMEM((ROWS, WIDTH), F32), pltpu.SemaphoreType.DMA((7,))],
        compiler_params=pltpu.CompilerParams(vmem_limit_bytes=2**23),
    )(*(pltpu.with_memory_space_constraint(x, pltpu.VMEM) for x in held))
    return outputs, new_w[:, None], new_one[:, None], new_two[:, None]


def solution(mesh):
    rows = P(("expert", "replica"), None)
    state = P(None, "expert", "replica", None)
    return jax.shard_map(
        on_device,
        mesh=mesh,
        in_specs=(rows, rows, rows, state, state, state),
        out_specs=(rows, state, state, state),
        check_vma=False,
    )
```

```python
import jax
import jax.numpy as jnp
from jax import lax
from jax.experimental import pallas as pl
from jax.experimental.pallas import tpu as pltpu
from jax.sharding import PartitionSpec as P

MESH = pl.DeviceIdType.MESH
CORR_ONE = 0.9999734386011124
CORR_TWO = 0.09520785288629038
F32 = jnp.float32
BF16 = jnp.bfloat16

SIDE = 4
PEERS = SIDE**3
CAP = 32
WIDTH = 256
ROWS = 1024
LAYERS = 7
HALF = WIDTH // 2
PER = 16
GROUPS = PEERS // PER
TILE = PER * CAP
PACK = 8
PACKS = PEERS // PACK
PACK_TILE = PACK * CAP
STRIDE = 27


def split(value):
    high = value.astype(BF16)
    low = (value - high.astype(F32)).astype(BF16)
    return high, low


def mm(a, b):
    return lax.dot_general(a, b, (((1,), (0,)), ((), ())), preferred_element_type=F32)


def mm_nt(a, b):
    return lax.dot_general(a, b, (((1,), (1,)), ((), ())), preferred_element_type=F32)


def mm_tn(a, b):
    return lax.dot_general(a, b, (((0,), (0,)), ((), ())), preferred_element_type=F32)


def peer(me, k):
    off = lax.rem(k * STRIDE, PEERS)
    x = lax.rem(me + off, SIDE)
    y = lax.rem(lax.div(me, SIDE) + lax.div(off, SIDE), SIDE)
    z = lax.rem(lax.div(me, SIDE * SIDE) + lax.div(off, SIDE * SIDE), SIDE)
    return z * (SIDE * SIDE) + y * SIDE + x


def peer_back(me, k):
    off = lax.rem(k * STRIDE, PEERS)
    x = lax.rem(me + SIDE - lax.rem(off, SIDE), SIDE)
    y = lax.rem(lax.div(me, SIDE) + SIDE - lax.rem(lax.div(off, SIDE), SIDE), SIDE)
    z = lax.rem(lax.div(me, SIDE * SIDE) + SIDE - lax.div(off, SIDE * SIDE), SIDE)
    return z * (SIDE * SIDE) + y * SIDE + x


def wanted(me, start, shape, axis):
    j = lax.broadcasted_iota(jnp.int32, shape, axis) + start
    k = lax.shift_right_logical(j, 5)
    off = (k * STRIDE) & (PEERS - 1)
    x = (me + off) & 3
    y = (lax.shift_right_logical(off, 2) + me // SIDE) & 3
    z = (lax.shift_right_logical(off, 4) + me // (SIDE * SIDE)) & 3
    return (z * 16 + y * 4 + x) * CAP + (j & (CAP - 1))


def kernel(
    routes, samples, cotangent, weights, one, two,
    ret, place, outputs, new_w, new_one, new_two,
    rv, sv, cv, wf, m1, m2, wh, wl, sp, cp, arr, arc, ah, al, slope, grads, got, slot, slot_t,
    in_sem, send_sem, recv_sem, w_sem, g_sem,
):
    me = lax.axis_index("expert")
    rep = lax.axis_index("replica")
    other = 1 - rep

    loads = [
        pltpu.make_async_copy(src, dst, in_sem.at[i])
        for i, (src, dst) in enumerate(
            ((samples, sv), (weights, wf.at[rep]), (cotangent, cv), (one, m1), (two, m2), (routes, rv))
        )
    ]
    loads[5].start()
    loads[0].start()

    barrier = pltpu.get_barrier_semaphore()
    at_x = lax.rem(me, SIDE)
    at_y = lax.rem(lax.div(me, SIDE), SIDE)
    at_z = lax.div(me, SIDE * SIDE)
    xs, ys, zs = (
        [at] + [lax.rem(at + step, SIDE) for step in range(1, SIDE)] for at in (at_x, at_y, at_z)
    )
    for off in range(PEERS - 1, 0, -1):
        z, y, x = zs[off // 16], ys[off // 4 % 4], xs[off % 4]
        to = z * (SIDE * SIDE) + y * SIDE + x
        pl.semaphore_signal(barrier, inc=1, device_id={"expert": to}, device_id_type=MESH)
    pl.semaphore_signal(barrier, inc=1, device_id={"replica": other}, device_id_type=MESH)

    loads[5].wait()
    route = rv[...]
    earlier = (
        lax.broadcasted_iota(jnp.int32, (256, 256), 0) < lax.broadcasted_iota(jnp.int32, (256, 256), 1)
    ).astype(F32).astype(BF16)
    experts = lax.broadcasted_iota(jnp.int32, (PEERS, 256), 0)
    base = jnp.zeros((PEERS, 1), F32)
    for b in range(ROWS // 256):
        part = route[:, b * 256 : (b + 1) * 256]
        hot = (experts == part).astype(F32)
        before = mm(hot.astype(BF16), earlier) + base
        rank = jnp.sum(hot * before, axis=0, keepdims=True)
        base = base + jnp.sum(hot, axis=1, keepdims=True)
        slot[:, b * 256 : (b + 1) * 256] = part * CAP + rank.astype(jnp.int32)

    def remote(phase, src, dst, k, to):
        return pltpu.make_async_remote_copy(
            src_ref=src, dst_ref=dst, send_sem=send_sem.at[phase], recv_sem=recv_sem.at[phase, k // PER],
            device_id={"expert": to}, device_id_type=MESH,
        )

    def send_range(phase, src, dst, start, count, where):
        @pl.when(start == 0)
        def _():
            pltpu.make_async_copy(src.at[0], dst.at[0], recv_sem.at[phase, 0]).start()

        @pl.when(start > 0)
        def _():
            remote(phase, src.at[start], dst.at[start], start, where(me, start)).start()

        def one_send(i, carry):
            k = start + i
            remote(phase, src.at[k], dst.at[k], k, where(me, k)).start()
            return carry

        lax.fori_loop(1, count, one_send, 0)

    def wait_group(phase, dst, g):
        block = dst.at[pl.ds(g * PER, PER)]
        remote(phase, block, block, g * PER, me).wait_recv()

    def pack_group(high, low, dst, g):
        want = wanted(me, g * PACK_TILE, (PACK_TILE, 128), 0)
        want = jnp.concatenate([want] * (ROWS // 128), axis=1)
        hot = (want == slot[...]).astype(F32).astype(BF16)
        packed = mm(hot, high) + mm(hot, low)
        dst[pl.ds(g * PACK, PACK)] = packed.reshape(PACK, CAP, WIDTH)

    loads[0].wait()
    s_high, s_low = split(sv[...])
    pack_group(s_high, s_low, sp, 0)
    pl.semaphore_wait(barrier, PEERS)
    send_range(0, sp, arr, 0, PACK, peer)
    for load in loads[1:5]:
        load.start()
    def pack_samples(g, carry):
        pack_group(s_high, s_low, sp, g)
        send_range(0, sp, arr, g * PACK, PACK, peer)
        return carry

    lax.fori_loop(1, PACKS, pack_samples, 0)

    loads[1].wait()
    weight_copy = pltpu.make_async_remote_copy(
        src_ref=wf.at[rep], dst_ref=wf.at[rep], send_sem=w_sem.at[0], recv_sem=w_sem.at[1],
        device_id={"replica": other}, device_id_type=MESH,
    )
    weight_copy.start()

    loads[2].wait()
    c_high, c_low = split(cv[...])

    def pack_cotangent(g, carry):
        pack_group(c_high, c_low, cp, g)
        send_range(1, cp, arc, g * PACK, PACK, peer)
        return carry

    lax.fori_loop(0, PACKS, pack_cotangent, 0)

    slot_t[...] = jnp.transpose(jnp.broadcast_to(slot[...], (128, ROWS)))

    def spread_rows(g, carry):
        want = wanted(me, g * TILE, (8, TILE), 1)[:1]

        def some_rows(i, carry):
            rows = pl.ds(i * 256, 256)
            mine = jnp.concatenate([slot_t[rows]] * (TILE // 128), axis=1)
            place[g, rows] = (mine == want).astype(F32).astype(BF16)
            return carry

        return lax.fori_loop(0, ROWS // 256, some_rows, carry)

    lax.fori_loop(0, GROUPS, spread_rows, 0)

    weight_copy.wait()

    def split_weights(layer, carry):
        for half in range(2):
            high, low = split(wf[half, layer])
            wh[layer, half * HALF : (half + 1) * HALF] = high
            wl[layer, half * HALF : (half + 1) * HALF] = low
        grads[0, layer] = jnp.zeros((HALF, WIDTH), F32)
        grads[1, layer] = jnp.zeros((HALF, WIDTH), F32)
        return carry

    lax.fori_loop(0, LAYERS, split_weights, 0)

    def forward(g, carry):
        wait_group(0, arr, g)
        rows = pl.ds(g * TILE, TILE)
        hidden = arr[pl.ds(g * PER, PER)].reshape(TILE, WIDTH)
        for layer in range(LAYERS):
            high, low = split(hidden)
            ah[layer, rows] = high
            al[layer, rows] = low
            pre = mm(high, wh[layer]) + mm(low, wh[layer]) + mm(high, wl[layer])
            if layer < LAYERS - 1:
                sigma = jax.nn.sigmoid(pre)
                hidden = pre * sigma
                slope[layer, rows] = sigma + hidden * (1.0 - sigma)
        arr[pl.ds(g * PER, PER)] = pre.reshape(PER, CAP, WIDTH)
        return carry

    lax.fori_loop(0, GROUPS, forward, 0)

    def backward(g, carry):
        wait_group(1, arc, g)
        rows = pl.ds(g * TILE, TILE)
        delta = arc[pl.ds(g * PER, PER)].reshape(TILE, WIDTH)
        for layer in range(LAYERS - 1, -1, -1):
            high, low = split(delta)
            a_high, a_low = ah[layer, rows], al[layer, rows]
            grad = mm_tn(a_high, high) + mm_tn(a_high, low) + mm_tn(a_low, high)
            grads[0, layer] += grad[:HALF]
            grads[1, layer] += grad[HALF:]
            if layer > 0:
                back = mm_nt(high, wh[layer]) + mm_nt(low, wh[layer]) + mm_nt(high, wl[layer])
                delta = back * slope[layer - 1, rows]
        return carry

    def unpack(g, first):
        wait_group(2, ret, g)
        high, low = split(ret[pl.ds(g * PER, PER)].reshape(TILE, WIDTH))

        def some_rows(i, carry):
            rows = pl.ds(i * 256, 256)
            hot = place[g, rows]
            found = mm(hot, high) + mm(hot, low)
            outputs[rows] = found if first else outputs[rows] + found
            return carry

        lax.fori_loop(0, ROWS // 256, some_rows, 0)

    def send_and_backward(g, carry):
        send_range(2, arr, ret, g * PER, PER, peer_back)
        return backward(g, carry)

    lax.fori_loop(0, GROUPS - 1, send_and_backward, 0)
    send_range(2, arr, ret, (GROUPS - 1) * PER, PER, peer_back)
    unpack(0, True)
    backward(GROUPS - 1, 0)

    grad_copy = pltpu.make_async_remote_copy(
        src_ref=grads.at[other], dst_ref=got, send_sem=g_sem.at[0], recv_sem=g_sem.at[1],
        device_id={"replica": other}, device_id_type=MESH,
    )
    grad_copy.start()
    unpack(1, False)
    loads[3].wait()
    loads[4].wait()
    grad_copy.wait()

    def adam(layer, carry):
        grad = grads[rep, layer] + got[layer]
        first = 0.9 * m1[layer] + 0.1 * grad
        second = 0.999 * m2[layer] + 0.001 * grad * grad
        new_one[layer] = first
        new_two[layer] = second
        new_w[layer] = wf[rep, layer] - 0.01 * (first / CORR_ONE) / (jnp.sqrt(second / CORR_TWO) + 1e-08)
        return carry

    lax.fori_loop(0, LAYERS, adam, 0)
    for g in range(2, GROUPS - 1):
        unpack(g, False)
    wait_group(2, ret, GROUPS - 1)

    for phase, src in enumerate((sp, cp, arr)):
        block = src.at[pl.ds(1, PEERS - 1)]
        remote(phase, block, block, 0, me).wait_send()


def finish(ret, place, partial, w, one, two, outputs, new_w, new_one, new_two, rows_out, sem):
    copies = [
        pltpu.make_async_copy(src, dst, sem.at[i])
        for i, (src, dst) in enumerate(((w, new_w), (one, new_one), (two, new_two)))
    ]
    for copy in copies:
        copy.start()
    high, low = split(ret[PEERS - PER :].reshape(TILE, WIDTH))
    part = 256
    for i in range(ROWS // part):
        rows = pl.ds(i * part, part)
        hot = place[GROUPS - 1, rows]
        rows_out[rows] = partial[rows] + mm(hot, high) + mm(hot, low)
        copies.append(pltpu.make_async_copy(rows_out.at[rows], outputs.at[rows], sem.at[3 + i]))
        copies[-1].start()
    for copy in copies:
        copy.wait()


def on_device(samples, routes, cotangent, weights, moment_one, moment_two):
    shard = (LAYERS, HALF, WIDTH)
    state = jax.ShapeDtypeStruct(shard, F32)
    hbm = pl.BlockSpec(memory_space=pl.ANY)
    vmem = pl.BlockSpec(memory_space=pltpu.VMEM)
    peers = (PEERS, CAP, WIDTH)
    slots = PEERS * CAP
    flops = 2 * slots * WIDTH * WIDTH * 60
    held = pl.pallas_call(
        kernel,
        out_shape=(
            pltpu.VMEM(peers, F32),
            pltpu.VMEM((GROUPS, ROWS, TILE), BF16),
            pltpu.VMEM((ROWS, WIDTH), F32),
            pltpu.VMEM(shard, F32),
            pltpu.VMEM(shard, F32),
            pltpu.VMEM(shard, F32),
        ),
        in_specs=[hbm] * 6,
        out_specs=(vmem,) * 6,
        scratch_shapes=[
            pltpu.VMEM((1, ROWS), jnp.int32),
            pltpu.VMEM((ROWS, WIDTH), F32),
            pltpu.VMEM((ROWS, WIDTH), F32),
            pltpu.VMEM((2,) + shard, F32),
            pltpu.VMEM(shard, F32),
            pltpu.VMEM(shard, F32),
            pltpu.VMEM((LAYERS, WIDTH, WIDTH), BF16),
            pltpu.VMEM((LAYERS, WIDTH, WIDTH), BF16),
            pltpu.VMEM(peers, F32),
            pltpu.VMEM(peers, F32),
            pltpu.VMEM(peers, F32),
            pltpu.VMEM(peers, F32),
            pltpu.VMEM((LAYERS, slots, WIDTH), BF16),
            pltpu.VMEM((LAYERS, slots, WIDTH), BF16),
            pltpu.VMEM((LAYERS - 1, slots, WIDTH), F32),
            pltpu.VMEM((2,) + shard, F32),
            pltpu.VMEM(shard, F32),
            pltpu.VMEM((1, ROWS), jnp.int32),
            pltpu.VMEM((ROWS, 128), jnp.int32),
            pltpu.SemaphoreType.DMA((6,)),
            pltpu.SemaphoreType.DMA((3,)),
            pltpu.SemaphoreType.DMA((3, GROUPS)),
            pltpu.SemaphoreType.DMA((2,)),
            pltpu.SemaphoreType.DMA((2,)),
        ],
        compiler_params=pltpu.CompilerParams(
            collective_id=0, has_side_effects=True, vmem_limit_bytes=50 * 2**20
        ),
        cost_estimate=pl.CostEstimate(flops=flops, bytes_accessed=2**23, transcendentals=slots * WIDTH * 6),
    )(
        routes.reshape(1, ROWS),
        samples,
        cotangent,
        weights[:, 0],
        moment_one[:, 0],
        moment_two[:, 0],
    )
    outputs, new_w, new_one, new_two = pl.pallas_call(
        finish,
        out_shape=(jax.ShapeDtypeStruct((ROWS, WIDTH), F32), state, state, state),
        in_specs=[vmem] * 6,
        out_specs=(hbm,) * 4,
        scratch_shapes=[pltpu.VMEM((ROWS, WIDTH), F32), pltpu.SemaphoreType.DMA((7,))],
        compiler_params=pltpu.CompilerParams(vmem_limit_bytes=2**23),
    )(*(pltpu.with_memory_space_constraint(x, pltpu.VMEM) for x in held))
    return outputs, new_w[:, None], new_one[:, None], new_two[:, None]


def solution(mesh):
    rows = P(("expert", "replica"), None)
    state = P(None, "expert", "replica", None)
    return jax.shard_map(
        on_device,
        mesh=mesh,
        in_specs=(rows, rows, rows, state, state, state),
        out_specs=(rows, state, state, state),
        check_vma=False,
    )
```

```python
import jax
import jax.numpy as jnp
from jax import lax
from jax.experimental import pallas as pl
from jax.experimental.pallas import tpu as pltpu
from jax.sharding import PartitionSpec as P

MESH = pl.DeviceIdType.MESH
CORR_ONE = 0.9999734386011124
CORR_TWO = 0.09520785288629038
F32 = jnp.float32
BF16 = jnp.bfloat16

SIDE = 4
PEERS = SIDE**3
CAP = 32
WIDTH = 256
ROWS = 1024
LAYERS = 7
HALF = WIDTH // 2
PER = 16
GROUPS = PEERS // PER
TILE = PER * CAP
PACK = 8
PACKS = PEERS // PACK
PACK_TILE = PACK * CAP
STRIDE = 19


def split(value):
    high = value.astype(BF16)
    low = (value - high.astype(F32)).astype(BF16)
    return high, low


def mm(a, b):
    return lax.dot_general(a, b, (((1,), (0,)), ((), ())), preferred_element_type=F32)


def mm_nt(a, b):
    return lax.dot_general(a, b, (((1,), (1,)), ((), ())), preferred_element_type=F32)


def mm_tn(a, b):
    return lax.dot_general(a, b, (((0,), (0,)), ((), ())), preferred_element_type=F32)


def peer(me, k, turn):
    off = lax.rem(k * STRIDE, PEERS)
    x = lax.rem(me + off * turn, SIDE)
    y = lax.rem(lax.div(me, SIDE) + lax.div(off, SIDE) * turn, SIDE)
    z = lax.rem(lax.div(me, SIDE * SIDE) + lax.div(off, SIDE * SIDE) * turn, SIDE)
    return z * (SIDE * SIDE) + y * SIDE + x


def wanted(me, turn, start, shape, axis):
    j = lax.broadcasted_iota(jnp.int32, shape, axis) + start
    k = lax.shift_right_logical(j, 5)
    off = (k * STRIDE) & (PEERS - 1)
    x = (me + off * turn) & 3
    y = (me // SIDE + lax.shift_right_logical(off, 2) * turn) & 3
    z = (me // (SIDE * SIDE) + lax.shift_right_logical(off, 4) * turn) & 3
    return (z * 16 + y * 4 + x) * CAP + (j & (CAP - 1))


def kernel(
    routes, samples, cotangent, weights, one, two,
    ret, place, outputs, new_w, new_one, new_two,
    rv, sv, cv, wf, m1, m2, wh, wl, sp, cp, arr, arc, ah, al, slope, grads, got, slot, slot_t,
    in_sem, send_sem, recv_sem, w_sem, g_sem,
):
    me = lax.axis_index("expert")
    rep = lax.axis_index("replica")
    other = 1 - rep
    turn = 1 + 2 * rep
    turn_back = 3 - 2 * rep

    loads = [
        pltpu.make_async_copy(src, dst, in_sem.at[i])
        for i, (src, dst) in enumerate(
            ((samples, sv), (weights, wf.at[rep]), (cotangent, cv), (one, m1), (two, m2), (routes, rv))
        )
    ]
    loads[5].start()
    loads[0].start()

    barrier = pltpu.get_barrier_semaphore()
    at_x = lax.rem(me, SIDE)
    at_y = lax.rem(lax.div(me, SIDE), SIDE)
    at_z = lax.div(me, SIDE * SIDE)
    xs, ys, zs = (
        [at] + [lax.rem(at + step, SIDE) for step in range(1, SIDE)] for at in (at_x, at_y, at_z)
    )
    for off in range(PEERS - 1, 0, -1):
        z, y, x = zs[off // 16], ys[off // 4 % 4], xs[off % 4]
        to = z * (SIDE * SIDE) + y * SIDE + x
        pl.semaphore_signal(barrier, inc=1, device_id={"expert": to}, device_id_type=MESH)
    pl.semaphore_signal(barrier, inc=1, device_id={"replica": other}, device_id_type=MESH)

    loads[5].wait()
    route = rv[...]
    earlier = (
        lax.broadcasted_iota(jnp.int32, (256, 256), 0) < lax.broadcasted_iota(jnp.int32, (256, 256), 1)
    ).astype(F32).astype(BF16)
    experts = lax.broadcasted_iota(jnp.int32, (PEERS, 256), 0)
    base = jnp.zeros((PEERS, 1), F32)
    for b in range(ROWS // 256):
        part = route[:, b * 256 : (b + 1) * 256]
        hot = (experts == part).astype(F32)
        before = mm(hot.astype(BF16), earlier) + base
        rank = jnp.sum(hot * before, axis=0, keepdims=True)
        base = base + jnp.sum(hot, axis=1, keepdims=True)
        slot[:, b * 256 : (b + 1) * 256] = part * CAP + rank.astype(jnp.int32)

    def remote(phase, src, dst, k, to):
        return pltpu.make_async_remote_copy(
            src_ref=src, dst_ref=dst, send_sem=send_sem.at[phase], recv_sem=recv_sem.at[phase, k // PER],
            device_id={"expert": to}, device_id_type=MESH,
        )

    def send_range(phase, src, dst, start, count, where):
        @pl.when(start == 0)
        def _():
            pltpu.make_async_copy(src.at[0], dst.at[0], recv_sem.at[phase, 0]).start()

        @pl.when(start > 0)
        def _():
            remote(phase, src.at[start], dst.at[start], start, peer(me, start, where)).start()

        def one_send(i, carry):
            k = start + i
            remote(phase, src.at[k], dst.at[k], k, peer(me, k, where)).start()
            return carry

        lax.fori_loop(1, count, one_send, 0)

    def wait_group(phase, dst, g):
        block = dst.at[pl.ds(g * PER, PER)]
        remote(phase, block, block, g * PER, me).wait_recv()

    def pack_group(high, low, dst, g):
        want = wanted(me, turn, g * PACK_TILE, (PACK_TILE, 128), 0)
        want = jnp.concatenate([want] * (ROWS // 128), axis=1)
        hot = (want == slot[...]).astype(F32).astype(BF16)
        packed = mm(hot, high) + mm(hot, low)
        dst[pl.ds(g * PACK, PACK)] = packed.reshape(PACK, CAP, WIDTH)

    loads[0].wait()
    s_high, s_low = split(sv[...])
    pack_group(s_high, s_low, sp, 0)
    pl.semaphore_wait(barrier, PEERS)
    send_range(0, sp, arr, 0, PACK, turn)
    for load in loads[1:5]:
        load.start()
    def pack_samples(g, carry):
        pack_group(s_high, s_low, sp, g)
        send_range(0, sp, arr, g * PACK, PACK, turn)
        return carry

    lax.fori_loop(1, PACKS, pack_samples, 0)

    loads[1].wait()
    weight_copy = pltpu.make_async_remote_copy(
        src_ref=wf.at[rep], dst_ref=wf.at[rep], send_sem=w_sem.at[0], recv_sem=w_sem.at[1],
        device_id={"replica": other}, device_id_type=MESH,
    )
    weight_copy.start()

    loads[2].wait()
    c_high, c_low = split(cv[...])

    def pack_cotangent(g, carry):
        pack_group(c_high, c_low, cp, g)
        send_range(1, cp, arc, g * PACK, PACK, turn)
        return carry

    lax.fori_loop(0, PACKS, pack_cotangent, 0)

    slot_t[...] = jnp.transpose(jnp.broadcast_to(slot[...], (128, ROWS)))

    def spread_rows(g, carry):
        want = wanted(me, turn, g * TILE, (8, TILE), 1)[:1]

        def some_rows(i, carry):
            rows = pl.ds(i * 256, 256)
            mine = jnp.concatenate([slot_t[rows]] * (TILE // 128), axis=1)
            place[g, rows] = (mine == want).astype(F32).astype(BF16)
            return carry

        return lax.fori_loop(0, ROWS // 256, some_rows, carry)

    lax.fori_loop(0, GROUPS, spread_rows, 0)

    weight_copy.wait()

    def split_weights(layer, carry):
        for half in range(2):
            high, low = split(wf[half, layer])
            wh[layer, half * HALF : (half + 1) * HALF] = high
            wl[layer, half * HALF : (half + 1) * HALF] = low
        grads[0, layer] = jnp.zeros((HALF, WIDTH), F32)
        grads[1, layer] = jnp.zeros((HALF, WIDTH), F32)
        return carry

    lax.fori_loop(0, LAYERS, split_weights, 0)

    def forward(g, carry):
        wait_group(0, arr, g)
        rows = pl.ds(g * TILE, TILE)
        hidden = arr[pl.ds(g * PER, PER)].reshape(TILE, WIDTH)
        for layer in range(LAYERS):
            high, low = split(hidden)
            ah[layer, rows] = high
            al[layer, rows] = low
            pre = mm(high, wh[layer]) + mm(low, wh[layer]) + mm(high, wl[layer])
            if layer < LAYERS - 1:
                sigma = jax.nn.sigmoid(pre)
                hidden = pre * sigma
                slope[layer, rows] = sigma + hidden * (1.0 - sigma)
        arr[pl.ds(g * PER, PER)] = pre.reshape(PER, CAP, WIDTH)
        return carry

    lax.fori_loop(0, GROUPS, forward, 0)

    def backward(g, carry):
        wait_group(1, arc, g)
        rows = pl.ds(g * TILE, TILE)
        delta = arc[pl.ds(g * PER, PER)].reshape(TILE, WIDTH)
        for layer in range(LAYERS - 1, -1, -1):
            high, low = split(delta)
            a_high, a_low = ah[layer, rows], al[layer, rows]
            grad = mm_tn(a_high, high) + mm_tn(a_high, low) + mm_tn(a_low, high)
            grads[0, layer] += grad[:HALF]
            grads[1, layer] += grad[HALF:]
            if layer > 0:
                back = mm_nt(high, wh[layer]) + mm_nt(low, wh[layer]) + mm_nt(high, wl[layer])
                delta = back * slope[layer - 1, rows]
        return carry

    def unpack(g, first):
        wait_group(2, ret, g)
        high, low = split(ret[pl.ds(g * PER, PER)].reshape(TILE, WIDTH))

        def some_rows(i, carry):
            rows = pl.ds(i * 256, 256)
            hot = place[g, rows]
            found = mm(hot, high) + mm(hot, low)
            outputs[rows] = found if first else outputs[rows] + found
            return carry

        lax.fori_loop(0, ROWS // 256, some_rows, 0)

    def send_and_backward(g, carry):
        send_range(2, arr, ret, g * PER, PER, turn_back)
        return backward(g, carry)

    lax.fori_loop(0, GROUPS - 1, send_and_backward, 0)
    send_range(2, arr, ret, (GROUPS - 1) * PER, PER, turn_back)
    unpack(0, True)
    backward(GROUPS - 1, 0)

    grad_copy = pltpu.make_async_remote_copy(
        src_ref=grads.at[other], dst_ref=got, send_sem=g_sem.at[0], recv_sem=g_sem.at[1],
        device_id={"replica": other}, device_id_type=MESH,
    )
    grad_copy.start()
    unpack(1, False)
    loads[3].wait()
    loads[4].wait()
    grad_copy.wait()

    def adam(layer, carry):
        grad = grads[rep, layer] + got[layer]
        first = 0.9 * m1[layer] + 0.1 * grad
        second = 0.999 * m2[layer] + 0.001 * grad * grad
        new_one[layer] = first
        new_two[layer] = second
        new_w[layer] = wf[rep, layer] - 0.01 * (first / CORR_ONE) / (jnp.sqrt(second / CORR_TWO) + 1e-08)
        return carry

    lax.fori_loop(0, LAYERS, adam, 0)
    for g in range(2, GROUPS - 1):
        unpack(g, False)
    wait_group(2, ret, GROUPS - 1)

    for phase, src in enumerate((sp, cp, arr)):
        block = src.at[pl.ds(1, PEERS - 1)]
        remote(phase, block, block, 0, me).wait_send()


def finish(ret, place, partial, w, one, two, outputs, new_w, new_one, new_two, rows_out, sem):
    copies = [
        pltpu.make_async_copy(src, dst, sem.at[i])
        for i, (src, dst) in enumerate(((w, new_w), (one, new_one), (two, new_two)))
    ]
    for copy in copies:
        copy.start()
    high, low = split(ret[PEERS - PER :].reshape(TILE, WIDTH))
    part = 256
    for i in range(ROWS // part):
        rows = pl.ds(i * part, part)
        hot = place[GROUPS - 1, rows]
        rows_out[rows] = partial[rows] + mm(hot, high) + mm(hot, low)
        copies.append(pltpu.make_async_copy(rows_out.at[rows], outputs.at[rows], sem.at[3 + i]))
        copies[-1].start()
    for copy in copies:
        copy.wait()


def on_device(samples, routes, cotangent, weights, moment_one, moment_two):
    shard = (LAYERS, HALF, WIDTH)
    state = jax.ShapeDtypeStruct(shard, F32)
    hbm = pl.BlockSpec(memory_space=pl.ANY)
    vmem = pl.BlockSpec(memory_space=pltpu.VMEM)
    peers = (PEERS, CAP, WIDTH)
    slots = PEERS * CAP
    flops = 2 * slots * WIDTH * WIDTH * 60
    held = pl.pallas_call(
        kernel,
        out_shape=(
            pltpu.VMEM(peers, F32),
            pltpu.VMEM((GROUPS, ROWS, TILE), BF16),
            pltpu.VMEM((ROWS, WIDTH), F32),
            pltpu.VMEM(shard, F32),
            pltpu.VMEM(shard, F32),
            pltpu.VMEM(shard, F32),
        ),
        in_specs=[hbm] * 6,
        out_specs=(vmem,) * 6,
        scratch_shapes=[
            pltpu.VMEM((1, ROWS), jnp.int32),
            pltpu.VMEM((ROWS, WIDTH), F32),
            pltpu.VMEM((ROWS, WIDTH), F32),
            pltpu.VMEM((2,) + shard, F32),
            pltpu.VMEM(shard, F32),
            pltpu.VMEM(shard, F32),
            pltpu.VMEM((LAYERS, WIDTH, WIDTH), BF16),
            pltpu.VMEM((LAYERS, WIDTH, WIDTH), BF16),
            pltpu.VMEM(peers, F32),
            pltpu.VMEM(peers, F32),
            pltpu.VMEM(peers, F32),
            pltpu.VMEM(peers, F32),
            pltpu.VMEM((LAYERS, slots, WIDTH), BF16),
            pltpu.VMEM((LAYERS, slots, WIDTH), BF16),
            pltpu.VMEM((LAYERS - 1, slots, WIDTH), F32),
            pltpu.VMEM((2,) + shard, F32),
            pltpu.VMEM(shard, F32),
            pltpu.VMEM((1, ROWS), jnp.int32),
            pltpu.VMEM((ROWS, 128), jnp.int32),
            pltpu.SemaphoreType.DMA((6,)),
            pltpu.SemaphoreType.DMA((3,)),
            pltpu.SemaphoreType.DMA((3, GROUPS)),
            pltpu.SemaphoreType.DMA((2,)),
            pltpu.SemaphoreType.DMA((2,)),
        ],
        compiler_params=pltpu.CompilerParams(
            collective_id=0, has_side_effects=True, vmem_limit_bytes=50 * 2**20
        ),
        cost_estimate=pl.CostEstimate(flops=flops, bytes_accessed=2**23, transcendentals=slots * WIDTH * 6),
    )(
        routes.reshape(1, ROWS),
        samples,
        cotangent,
        weights[:, 0],
        moment_one[:, 0],
        moment_two[:, 0],
    )
    outputs, new_w, new_one, new_two = pl.pallas_call(
        finish,
        out_shape=(jax.ShapeDtypeStruct((ROWS, WIDTH), F32), state, state, state),
        in_specs=[vmem] * 6,
        out_specs=(hbm,) * 4,
        scratch_shapes=[pltpu.VMEM((ROWS, WIDTH), F32), pltpu.SemaphoreType.DMA((7,))],
        compiler_params=pltpu.CompilerParams(vmem_limit_bytes=2**23),
    )(*(pltpu.with_memory_space_constraint(x, pltpu.VMEM) for x in held))
    return outputs, new_w[:, None], new_one[:, None], new_two[:, None]


def solution(mesh):
    rows = P(("expert", "replica"), None)
    state = P(None, "expert", "replica", None)
    return jax.shard_map(
        on_device,
        mesh=mesh,
        in_specs=(rows, rows, rows, state, state, state),
        out_specs=(rows, state, state, state),
        check_vma=False,
    )
```
